256 devices in a mesh: fsdp: 2 (over y_hi), rows: 16 (over z, core), cols: 8 (over y_lo, x).
Axes of the slice: x: 4, y: 4 (y_hi: 2, y_lo: 2; y = y_hi * 2 + y_lo), z: 8, core: 2. Of those that a mesh axis runs over, the one named last changes fastest.
Arguments:
- image: bfloat16 [2, 256, 1024, 128], P('fsdp', 'rows', 'cols'), may hold values from -6 to 6
- dw_kernel: float32 [7, 7, 128], replicated, may hold values from -0.875 to 0.875
- dw_bias: float32 [128], replicated, may hold values from -3 to 3
- layer_norm_gain: float32 [128], replicated, may hold values from 0.1 to 1.9
- layer_norm_bias: float32 [128], replicated, may hold values from -3 to 3
- w_in: bfloat16 [128, 512], P('fsdp'), may hold values from -0.5 to 0.5
- b_in: float32 [512], replicated, may hold values from -3 to 3
- w_out: bfloat16 [512, 128], P('fsdp'), may hold values from -0.25 to 0.25
- b_out: float32 [128], replicated, may hold values from -3 to 3
- cotangent: bfloat16 [2, 256, 1024, 128], P('fsdp', 'rows', 'cols'), may hold values from -60 to 60
Outputs:
- mixed: bfloat16 [2, 256, 1024, 128], P('fsdp', 'rows', 'cols')
- d_image: bfloat16 [2, 256, 1024, 128], P('fsdp', 'rows', 'cols')
- g_w_in: float32 [128, 512], P('fsdp')
- g_w_out: float32 [512, 128], P('fsdp')
- g_b_in: float32 [512], replicated
- g_kernel: float32 [7, 7, 128], replicated
- g_gain: float32 [128], replicated
The draws below stay inside these ranges and needn't reach their ends.
All inputs are finite; a program needn't handle non-finite values.
Results may differ from the reference program's by a relative error of at most 0.0057.
Values may be sent and summed in bfloat16 or wider, within the bound.
A program may use at most 64 MiB of HBM per device.

```python
import math
import jax
import jax.numpy as jnp
from jax import lax

C = 128
HID = 512
RH = 16
IMAGES = 2
H = 256
W = 1024
N_ROWS = 16


def draw_cotangent(key, part):
    keys = jax.random.split(key, 3)
    shape = (IMAGES, H, W, C)
    base = jnp.clip(jax.random.normal(keys[0], shape, jnp.float32), -6.0, 6.0)
    row_scale = 0.3 * jnp.exp(jax.random.uniform(keys[1], (IMAGES, H, 1, 1), jnp.float32) * math.log(10.0))
    col_scale = 0.3 * jnp.exp(jax.random.uniform(keys[2], (IMAGES, 1, W, 1), jnp.float32) * math.log(10.0))
    return (base * row_scale * col_scale).astype(jnp.bfloat16)


def shard_levels(rng, extent, cuts, least, largest):
    factor_of = 1.0
    for position, blocks in cuts:
        draws = jax.random.uniform(jax.random.fold_in(jax.random.fold_in(rng, 6), position), (blocks,), jnp.float32, least / len(cuts), largest / len(cuts))
        factor_of = factor_of * jnp.repeat(jnp.exp(draws), extent[position] // blocks).reshape((-1,) + (1,) * (len(extent) - 1 - position))
    return factor_of


def normal_values(key, shape, spread, reach, shards=(), dtype=jnp.bfloat16):
    gain = shard_levels(key, shape, shards, -0.22, 0.18) if shards else 1.0
    entries = jax.random.normal(key, shape, jnp.float32) * spread * gain
    return jnp.minimum(jnp.maximum(entries, -reach), reach).astype(dtype)


def setup_inputs(seed: int = 0) -> dict:
    splits = jax.random.split(jax.random.key(seed), 11)
    image = normal_values(splits[0], (IMAGES, H, W, C), 1.0, 6.0, ((0, 2), (1, 16), (2, 8)))
    dw_kernel = normal_values(splits[1], (7, 7, C), 49 ** -0.5, 0.875, (), jnp.float32)
    dw_bias = normal_values(splits[2], (C,), 0.5, 3.0, (), jnp.float32)
    layer_norm_gain = jnp.clip(1.0 + 0.18 * jax.random.normal(splits[3], (C,), jnp.float32), 0.1, 1.9)
    layer_norm_bias = normal_values(splits[4], (C,), 0.5, 3.0, (), jnp.float32)
    w_in = normal_values(splits[5], (C, HID), C ** -0.5, 0.5, ((0, 2),))
    b_in = normal_values(splits[6], (HID,), 0.5, 3.0, (), jnp.float32)
    w_out = normal_values(splits[7], (HID, C), HID ** -0.5, 0.25, ((0, 2),))
    b_out = normal_values(splits[8], (C,), 0.5, 3.0, (), jnp.float32)
    cotangent = draw_cotangent(jax.random.fold_in(splits[10], 71), 0)
    return dict(image=image, dw_kernel=dw_kernel, dw_bias=dw_bias, layer_norm_gain=layer_norm_gain, layer_norm_bias=layer_norm_bias, w_in=w_in, b_in=b_in, w_out=w_out, b_out=b_out, cotangent=cotangent)


norm_eps = 1e-06
gelu_coef = math.sqrt(2.0 / math.pi)
cubic_coef = 0.044715

def depthwise_taps(padded, kernel, height, width):
    total = jnp.zeros((height, width, padded.shape[2]), jnp.float32)
    for row_tap in range(7):
        for col_tap in range(7):
            total = total + padded[row_tap:row_tap + height, col_tap:col_tap + width] * kernel[row_tap, col_tap]
    return total

def transposed_taps(padded, kernel, height, width):
    total = jnp.zeros((height, width, padded.shape[2]), jnp.float32)
    for row_tap in range(7):
        for col_tap in range(7):
            total = total + padded[6 - row_tap:6 - row_tap + height, 6 - col_tap:6 - col_tap + width] * kernel[row_tap, col_tap]
    return total

def gelu_parts(pre):
    inner = gelu_coef * (pre + cubic_coef * pre * pre * pre)
    tanh_val = jnp.tanh(inner)
    value = 0.5 * pre * (1.0 + tanh_val)
    slope = 0.5 * (1.0 + tanh_val) + 0.5 * pre * (1.0 - tanh_val * tanh_val) * gelu_coef * (1.0 + 3.0 * cubic_coef * pre * pre)
    return (value, slope)

def reference(image, dw_kernel, dw_bias, layer_norm_gain, layer_norm_bias, w_in, b_in, w_out, b_out, cotangent):
    contract_rows = (((0,), (0,)), ((), ()))
    contract_cols = (((1,), (1,)), ((), ()))

    def per_image(pair):
        field, upstream = pair
        padded_f = jnp.pad(field.astype(jnp.float32), ((3, 3), (3, 3), (0, 0)))
        conv = depthwise_taps(padded_f, dw_kernel, H, W) + dw_bias
        center = lax.optimization_barrier(jnp.mean(conv, axis=-1, keepdims=True))
        variance_spread = conv - center
        inverse_deviation = lax.rsqrt(lax.optimization_barrier(jnp.mean(variance_spread * variance_spread, axis=-1, keepdims=True)) + norm_eps)
        standardized_input = variance_spread * inverse_deviation
        normalized_input = (standardized_input * layer_norm_gain + layer_norm_bias).astype(jnp.bfloat16)

        def per_block(block):
            normed_b, field_b, up_b = block
            pre = jnp.dot(normed_b, w_in, preferred_element_type=jnp.float32) + b_in
            value, slope = gelu_parts(pre)
            hidden = value.astype(jnp.bfloat16)
            mixed_b = (field_b.astype(jnp.float32) + jnp.dot(hidden, w_out, preferred_element_type=jnp.float32) + b_out).astype(jnp.bfloat16)
            d_hidden = lax.dot_general(up_b, w_out, contract_cols, preferred_element_type=jnp.float32)
            d_pre = (d_hidden * slope).astype(jnp.bfloat16)
            normalized_gradient = lax.dot_general(d_pre, w_in, contract_cols, preferred_element_type=jnp.float32)
            term_in = lax.dot_general(normed_b, d_pre, contract_rows, preferred_element_type=jnp.float32)
            term_out = lax.dot_general(hidden, up_b, contract_rows, preferred_element_type=jnp.float32)
            term_bias = lax.optimization_barrier(jnp.sum(d_pre.astype(jnp.float32), axis=0))
            return (mixed_b, normalized_gradient, term_in, term_out, term_bias)
        blocks = lax.map(per_block, (normalized_input.reshape(N_ROWS, RH * W, C), field.reshape(N_ROWS, RH * W, C), upstream.reshape(N_ROWS, RH * W, C)))
        mixed = blocks[0].reshape(H, W, C)
        normalized_gradient = blocks[1].reshape(H, W, C)
        gain_product = lax.optimization_barrier(jnp.sum(normalized_gradient * standardized_input, axis=(0, 1)))
        centered_scaled_gradient = normalized_gradient * layer_norm_gain
        convolution_gradient = (inverse_deviation * (centered_scaled_gradient - lax.optimization_barrier(jnp.mean(centered_scaled_gradient, axis=-1, keepdims=True)) - standardized_input * lax.optimization_barrier(jnp.mean(centered_scaled_gradient * standardized_input, axis=-1, keepdims=True)))).astype(jnp.bfloat16)
        conv_grad = convolution_gradient.astype(jnp.float32)
        grad_padded = jnp.pad(conv_grad, ((3, 3), (3, 3), (0, 0)))
        d_image = (upstream.astype(jnp.float32) + transposed_taps(grad_padded, dw_kernel, H, W)).astype(jnp.bfloat16)
        kernel_rows = []
        for row_tap in range(7):
            for col_tap in range(7):
                kernel_rows.append(lax.optimization_barrier(jnp.sum(padded_f[row_tap:row_tap + H, col_tap:col_tap + W] * conv_grad, axis=(0, 1))))
        kernel_term = jnp.stack(kernel_rows).reshape(7, 7, C)
        return (mixed, d_image, lax.optimization_barrier(jnp.sum(blocks[2], axis=0)), lax.optimization_barrier(jnp.sum(blocks[3], axis=0)), lax.optimization_barrier(jnp.sum(blocks[4], axis=0)), kernel_term, gain_product)
    results = lax.map(per_image, (image, cotangent))
    return (results[0], results[1], lax.optimization_barrier(jnp.sum(results[2], axis=0)), lax.optimization_barrier(jnp.sum(results[3], axis=0)), lax.optimization_barrier(jnp.sum(results[4], axis=0)), lax.optimization_barrier(jnp.sum(results[5], axis=0)), lax.optimization_barrier(jnp.sum(results[6], axis=0)))
```

```python
import functools
import math

import jax
import jax.numpy as jnp
from jax import lax
from jax.experimental import pallas as pl
from jax.experimental.pallas import tpu as pltpu
from jax.sharding import PartitionSpec as P

MESH = pl.DeviceIdType.MESH
F32 = jnp.float32
BF16 = jnp.bfloat16

norm_eps = 1e-06
gelu_coef = math.sqrt(2.0 / math.pi)
cubic_coef = 0.044715

RH = 16
CW = 128
C = 128
HID = 512
XY = 16
NR = 16
NC = 8
BLOCK = 256
NBLOCKS = RH * CW // BLOCK

NT = (((1,), (1,)), ((), ()))
TN = (((0,), (0,)), ((), ()))


def tap_sums(source, first, rows, taps, acc, kb, flip):
    for b in range(7):
        weights = [kb[(6 - a) * 8 + (6 - b) if flip else a * 8 + b] for a in range(7)]
        for row in rows:
            value = source[row, pl.ds(first + 5 + b, 8), :]
            for h, a in taps(row):
                acc[h] = acc[h] + value * weights[a]
    return acc


def taps_all(row):
    return [(row - a, a) for a in range(7) if 0 <= row - a < RH]


def kernel(
    image, dw_kernel, dw_bias, gain, bias, w_in, b_in, w_out, b_out, cotangent,
    mixed_out, d_image_out, g_in_out, g_out_out, g_b_out, g_k_out, g_gain_out,
    img, cot, xp, dp, cv, kb, win, wout, mixed, dcb, dimg,
    gwi, gwo, bacc, gacc, kacc,
    hx_row, hx_col, hx_cor, hd_row, hd_col, hd_cor,
    grads, r1, small, r1s, s2, r2, a4, sa,
    local_sem, w_send, w_recv, hx_send, hx_recv, hd_send, hd_recv,
    s1_send, s1_recv, s1s_send, s1s_recv, s2_send, s2_recv, s3_send, s3_recv, s4_send, s4_recv, s4s_send, s4s_recv,
):
    mf = lax.axis_index("fsdp")
    mr = lax.axis_index("rows")
    mc = lax.axis_index("cols")
    me = mf * NC + mc

    def xy_id(peer):
        return (peer // NC, mr, peer % NC)

    def row_id(peer):
        return (mf, peer, mc)

    up, down = (mr + NR - 1) % NR, (mr + 1) % NR
    left, right = (mc + NC - 1) % NC, (mc + 1) % NC

    load_image = pltpu.make_async_copy(image, img, local_sem.at[0])
    load_image.start()
    load_cot = pltpu.make_async_copy(cotangent, cot, local_sem.at[1])
    load_cot.start()
    load_in = pltpu.make_async_copy(w_in, win.at[pl.ds(mf * 64, 64)], local_sem.at[2])
    load_in.start()
    load_out = pltpu.make_async_copy(w_out, wout.at[pl.ds(mf * 256, 256)], local_sem.at[3])
    load_out.start()

    barrier = pltpu.get_barrier_semaphore()

    def greet_xy(k, _):
        pl.semaphore_signal(barrier, inc=1, device_id=xy_id((me + k) % XY), device_id_type=MESH)
        return 0

    def greet_rows(k, _):
        pl.semaphore_signal(barrier, inc=1, device_id=row_id((mr + k) % NR), device_id_type=MESH)
        return 0

    corners = ((up, left), (up, right), (down, left), (down, right))
    for r, c in corners:
        pl.semaphore_signal(barrier, inc=1, device_id=(mf, r, c), device_id_type=MESH)
    lax.fori_loop(1, XY, greet_xy, 0)
    lax.fori_loop(1, NR, greet_rows, 0)
    pl.semaphore_wait(barrier, 4 + XY - 1 + NR - 1)

    def halo(source, rows_buf, col_buf, cor_buf, send, recv):
        plan = [
            (source.at[pl.ds(RH - 3, 3)], rows_buf.at[0], (mf, down, mc)),
            (source.at[pl.ds(0, 3)], rows_buf.at[1], (mf, up, mc)),
            (source.at[:, pl.ds(CW - 16, 16)], col_buf.at[0], (mf, mr, right)),
            (source.at[:, pl.ds(0, 16)], col_buf.at[1], (mf, mr, left)),
            (source.at[pl.ds(RH - 3, 3), pl.ds(CW - 16, 16)], cor_buf.at[0], (mf, down, right)),
            (source.at[pl.ds(RH - 3, 3), pl.ds(0, 16)], cor_buf.at[1], (mf, down, left)),
            (source.at[pl.ds(0, 3), pl.ds(CW - 16, 16)], cor_buf.at[2], (mf, up, right)),
            (source.at[pl.ds(0, 3), pl.ds(0, 16)], cor_buf.at[3], (mf, up, left)),
        ]
        copies = []
        for i, (src, dst, target) in enumerate(plan):
            copy = pltpu.make_async_remote_copy(
                src_ref=src, dst_ref=dst, send_sem=send.at[i], recv_sem=recv.at[i], device_id=target, device_id_type=MESH
            )
            copy.start()
            copies.append(copy)
        return copies

    has_up = jnp.where(mr > 0, 1.0, 0.0).astype(F32)
    has_down = jnp.where(mr < NR - 1, 1.0, 0.0).astype(F32)
    has_left = jnp.where(mc > 0, 1.0, 0.0).astype(F32)
    has_right = jnp.where(mc < NC - 1, 1.0, 0.0).astype(F32)

    def unpack_halo(padded, rows_buf, col_buf, cor_buf):
        for i in range(3):
            padded[i, pl.ds(8, CW), :] = rows_buf[0, i].astype(F32) * has_up
            padded[RH + 3 + i, pl.ds(8, CW), :] = rows_buf[1, i].astype(F32) * has_down
            padded[i, pl.ds(0, 8), :] = cor_buf[0, i].astype(F32)[8:16] * (has_up * has_left)
            padded[i, pl.ds(CW + 8, 8), :] = cor_buf[1, i].astype(F32)[0:8] * (has_up * has_right)
            padded[RH + 3 + i, pl.ds(0, 8), :] = cor_buf[2, i].astype(F32)[8:16] * (has_down * has_left)
            padded[RH + 3 + i, pl.ds(CW + 8, 8), :] = cor_buf[3, i].astype(F32)[0:8] * (has_down * has_right)

        def side(r, _):
            padded[3 + r, pl.ds(0, 8), :] = col_buf[0, r].astype(F32)[8:16] * has_left
            padded[3 + r, pl.ds(CW + 8, 8), :] = col_buf[1, r].astype(F32)[0:8] * has_right
            return 0

        lax.fori_loop(0, RH, side, 0)

    hx = halo(image, hx_row, hx_col, hx_cor, hx_send, hx_recv)
    partner = (1 - mf, mr, mc)
    send_in = pltpu.make_async_remote_copy(
        src_ref=w_in, dst_ref=win.at[pl.ds(mf * 64, 64)], send_sem=w_send.at[0], recv_sem=w_recv.at[0],
        device_id=partner, device_id_type=MESH,
    )
    send_in.start()
    send_out = pltpu.make_async_remote_copy(
        src_ref=w_out, dst_ref=wout.at[pl.ds(mf * 256, 256)], send_sem=w_send.at[1], recv_sem=w_recv.at[1],
        device_id=partner, device_id_type=MESH,
    )
    send_out.start()

    for a in range(7):
        for b in range(7):
            kb[a * 8 + b] = jnp.broadcast_to(dw_kernel[a, pl.ds(b, 1), :], (8, C))
    conv_bias = jnp.broadcast_to(dw_bias[...], (8, C))

    load_image.wait()

    def widen(r, _):
        xp[3 + r, pl.ds(8, CW), :] = img[r].astype(F32)
        return 0

    lax.fori_loop(0, RH, widen, 0)

    own_rows = range(3, RH + 3)
    edge_rows = (0, 1, 2, RH + 3, RH + 4, RH + 5)

    def conv_inner(wb, _):
        first = pl.multiple_of(wb * 8, 8)
        acc = tap_sums(xp, first, own_rows, taps_all, [conv_bias] * RH, kb, False)
        for h in range(RH):
            cv[h, pl.ds(first, 8), :] = acc[h]
        return 0

    lax.fori_loop(1, CW // 8 - 1, conv_inner, 0)

    for copy in hx:
        copy.wait_recv()
    unpack_halo(xp, hx_row, hx_col, hx_cor)

    def conv_edge(wb, _):
        first = pl.multiple_of(wb * 8, 8)
        acc = [None] * RH
        touched = (0, 1, 2, RH - 3, RH - 2, RH - 1)
        for h in touched:
            acc[h] = cv[h, pl.ds(first, 8), :]
        acc = tap_sums(xp, first, edge_rows, taps_all, acc, kb, False)
        for h in touched:
            cv[h, pl.ds(first, 8), :] = acc[h]
        return 0

    lax.fori_loop(1, CW // 8 - 1, conv_edge, 0)

    def conv_side(i, _):
        first = pl.multiple_of(i * (CW - 8), 8)
        acc = tap_sums(xp, first, range(RH + 6), taps_all, [conv_bias] * RH, kb, False)
        for h in range(RH):
            cv[h, pl.ds(first, 8), :] = acc[h]
        return 0

    lax.fori_loop(0, 2, conv_side, 0)

    load_in.wait()
    load_out.wait()
    load_cot.wait()
    send_in.wait_recv()
    send_out.wait_recv()
    gwi[...] = jnp.zeros_like(gwi)
    gwo[...] = jnp.zeros_like(gwo)
    bacc[...] = jnp.zeros_like(bacc)
    gacc[...] = jnp.zeros_like(gacc)
    rows_per = BLOCK // CW

    def pointwise(i, _):
        r0 = i * rows_per
        conv = cv[pl.ds(r0, rows_per)].reshape(BLOCK, C)
        center = jnp.mean(conv, axis=-1, keepdims=True)
        spread = conv - center
        rstd = lax.rsqrt(jnp.mean(spread * spread, axis=-1, keepdims=True) + norm_eps)
        xhat = spread * rstd
        normed = (xhat * gain[...] + bias[...]).astype(BF16)
        up_b = cot[pl.ds(r0, rows_per)].reshape(BLOCK, C)
        out_sum = jnp.zeros((BLOCK, C), F32)
        dn = jnp.zeros((BLOCK, C), F32)
        half = HID // 2
        for j in range(2):
            cols = slice(j * half, (j + 1) * half)
            pre = jnp.dot(normed, win[:, cols], preferred_element_type=F32) + b_in[:, cols]
            square = pre * pre
            tanh_val = jnp.tanh(pre * (gelu_coef + (gelu_coef * cubic_coef) * square))
            half_gate = 0.5 + 0.5 * tanh_val
            hidden = (pre * half_gate).astype(BF16)
            slope = half_gate + (pre * (0.5 - 0.5 * tanh_val * tanh_val)) * (
                gelu_coef + (3.0 * gelu_coef * cubic_coef) * square
            )
            d_hidden = lax.dot_general(up_b, wout[cols, :], NT, preferred_element_type=F32)
            d_wide = d_hidden * slope
            d_pre = d_wide.astype(BF16)
            bacc[:, cols] += jnp.sum(d_wide.reshape(BLOCK // 8, 8, half), axis=0)
            out_sum = out_sum + jnp.dot(hidden, wout[cols, :], preferred_element_type=F32)
            dn = dn + lax.dot_general(d_pre, win[:, cols], NT, preferred_element_type=F32)
            gwi[:, cols] += lax.dot_general(normed, d_pre, TN, preferred_element_type=F32)
            gwo[:, cols] += lax.dot_general(up_b, hidden, TN, preferred_element_type=F32)
        field = img[pl.ds(r0, rows_per)].reshape(BLOCK, C).astype(F32)
        mixed[pl.ds(r0, rows_per)] = (field + out_sum + b_out[...]).astype(BF16).reshape(rows_per, CW, C)
        gacc[...] += jnp.sum((dn * xhat).reshape(BLOCK // 8, 8, C), axis=0)
        q = dn * gain[...]
        d_conv = (
            rstd * (q - jnp.mean(q, axis=-1, keepdims=True) - xhat * jnp.mean(q * xhat, axis=-1, keepdims=True))
        ).astype(BF16)
        d_rows = d_conv.reshape(rows_per, CW, C)
        dcb[pl.ds(r0, rows_per)] = d_rows
        dp[pl.ds(3 + r0, rows_per), pl.ds(8, CW), :] = d_rows.astype(F32)
        return 0

    lax.fori_loop(0, NBLOCKS, pointwise, 0)

    hd = halo(dcb, hd_row, hd_col, hd_cor, hd_send, hd_recv)
    save_mixed = pltpu.make_async_copy(mixed, mixed_out, local_sem.at[4])
    save_mixed.start()

    for q in range(4):
        turned = gwo[:, q * 128 : (q + 1) * 128].T
        for u in range(16):
            tile = turned[u * 8 : (u + 1) * 8]
            at = q * 4 + u // 4
            grads[at, 8 + 2 * (u % 4)] = tile[0:4]
            grads[at, 9 + 2 * (u % 4)] = tile[4:8]

    def deal(p, _):
        rows = gwi[pl.ds(pl.multiple_of(p * 8, 8), 8), :]
        for q in range(4):
            tile = rows[:, q * 128 : (q + 1) * 128]
            grads[p, 2 * q] = tile[0:4]
            grads[p, 2 * q + 1] = tile[4:8]
        return 0

    lax.fori_loop(0, XY, deal, 0)

    def copy_1(k):
        peer = (me + k) % XY
        return pltpu.make_async_remote_copy(
            src_ref=grads.at[peer], dst_ref=r1.at[k], send_sem=s1_send.at[k], recv_sem=s1_recv.at[k],
            device_id=xy_id(peer), device_id_type=MESH,
        )

    def copy_1s(k):
        peer = (me + k) % XY
        return pltpu.make_async_remote_copy(
            src_ref=small.at[peer], dst_ref=r1s.at[k], send_sem=s1s_send.at[k], recv_sem=s1s_recv.at[k],
            device_id=xy_id(peer), device_id_type=MESH,
        )

    def copy_2(k):
        peer = (mr + k) % NR
        return pltpu.make_async_remote_copy(
            src_ref=s2.at[peer], dst_ref=r2.at[mr], send_sem=s2_send.at[k], recv_sem=s2_recv.at[k],
            device_id=row_id(peer), device_id_type=MESH,
        )

    def copy_3(k):
        peer = (mr + k) % NR
        return pltpu.make_async_remote_copy(
            src_ref=a4.at[mc, mr], dst_ref=a4.at[mc, mr], send_sem=s3_send.at[k], recv_sem=s3_recv.at[k],
            device_id=row_id(peer), device_id_type=MESH,
        )

    def copy_4(k):
        return pltpu.make_async_remote_copy(
            src_ref=a4.at[mc], dst_ref=a4.at[mc], send_sem=s4_send.at[k], recv_sem=s4_recv.at[k],
            device_id=(mf, mr, (mc + k) % NC), device_id_type=MESH,
        )

    def copy_4s(k):
        return pltpu.make_async_remote_copy(
            src_ref=sa.at[me], dst_ref=sa.at[me], send_sem=s4s_send.at[k], recv_sem=s4s_recv.at[k],
            device_id=xy_id((me + k) % XY), device_id_type=MESH,
        )

    def each(count, act):
        def step(k, _):
            act(k)
            return 0

        lax.fori_loop(1, count, step, 0)

    each(XY, lambda k: copy_1(k).start())

    def tap_gradient(b):
        def step(wb, acc):
            first = pl.multiple_of(wb * 8, 8)
            acc = list(acc)
            grad = [dp[3 + h, pl.ds(first + 8, 8), :] for h in range(RH)]
            for row in range(RH + 6):
                value = xp[row, pl.ds(first + 5 + b, 8), :]
                for h, a in taps_all(row):
                    acc[a] = acc[a] + value * grad[h]
            return tuple(acc)

        acc = lax.fori_loop(0, CW // 8, step, tuple(jnp.zeros((8, C), F32) for _ in range(7)))
        for a in range(7):
            kacc[pl.ds((a * 8 + b) * 8, 8), :] = acc[a]

    for b in range(7):
        tap_gradient(b)
    for a in range(7):
        kacc[pl.ds((a * 8 + 7) * 8, 8), :] = jnp.zeros((8, C), F32)
    for a in range(7):
        total = kacc[pl.ds(a * 64, 8, stride=8), :]
        for s in range(1, 8):
            total = total + kacc[pl.ds(a * 64 + s, 8, stride=8), :]
        small[2 * a] = total[0:4]
        small[2 * a + 1] = total[4:8]
    for q in range(4):
        small[14, pl.ds(q, 1), :] = jnp.sum(bacc[:, q * 128 : (q + 1) * 128], axis=0, keepdims=True)
    small[15] = jnp.broadcast_to(jnp.sum(gacc[...], axis=0, keepdims=True), (4, C))
    each(XY, lambda k: copy_1s(k).start())

    for copy in hd:
        copy.wait_recv()
    unpack_halo(dp, hd_row, hd_col, hd_cor)

    def image_gradient(wb, _):
        first = pl.multiple_of(wb * 8, 8)
        acc = tap_sums(dp, first, range(RH + 6), taps_all, [jnp.zeros((8, C), F32)] * RH, kb, True)
        for h in range(RH):
            cv[h, pl.ds(first, 8), :] = acc[h]
        return 0

    lax.fori_loop(0, 8, image_gradient, 0)

    each(XY, lambda k: copy_1(k).wait_recv())
    each(XY, lambda k: copy_1s(k).wait_recv())
    little = small[me]
    for k in range(1, XY):
        little = little + r1s[k]

    def sum_1(r, _):
        total = grads[me, r]
        for k in range(1, XY):
            total = total + r1[k, r]
        s2[r, 0] = total
        s2[r, 1] = little
        return 0

    lax.fori_loop(0, NR, sum_1, 0)
    each(NR, lambda k: copy_2(k).start())
    r2[mr] = s2[mr]

    lax.fori_loop(8, 12, image_gradient, 0)

    each(NR, lambda k: copy_2(k).wait_recv())
    total = r2[0]
    for s in range(1, NR):
        total = total + r2[s]
    a4[mc, mr] = total[0]
    sa[me] = total[1]
    each(NR, lambda k: copy_3(k).start())
    each(XY, lambda k: copy_4s(k).start())

    lax.fori_loop(12, 16, image_gradient, 0)

    each(NR, lambda k: copy_3(k).wait_recv())
    each(NC, lambda k: copy_4(k).start())

    def finish(r, _):
        dimg[r] = (cot[r].astype(F32) + cv[r]).astype(BF16)
        return 0

    lax.fori_loop(0, RH, finish, 0)
    save_grad = pltpu.make_async_copy(dimg, d_image_out, local_sem.at[5])
    save_grad.start()

    each(XY, lambda k: copy_4s(k).wait_recv())
    for a in range(7):
        g_k_out[a, pl.ds(0, 4), :] = sa[2 * a]
        g_k_out[a, pl.ds(4, 3), :] = sa[2 * a + 1][0:3]
    for q in range(4):
        g_b_out[:, q * 128 : (q + 1) * 128] = sa[14, pl.ds(q, 1), :]
    g_gain_out[...] = sa[15, pl.ds(0, 1), :]

    each(NC, lambda k: copy_4(k).wait_recv())

    def place(j, _):
        for q in range(4):
            at = pl.multiple_of(j * 8, 8)
            g_in_out[pl.ds(at, 8), q * 128 : (q + 1) * 128] = jnp.concatenate([a4[j, 2 * q], a4[j, 2 * q + 1]], axis=0)
            at = pl.multiple_of(j * 32 + q * 8, 8)
            g_out_out[pl.ds(at, 8), :] = jnp.concatenate([a4[j, 8 + 2 * q], a4[j, 9 + 2 * q]], axis=0)
        return 0

    lax.fori_loop(0, NC, place, 0)

    for copy in hx:
        copy.wait_send()
    for copy in hd:
        copy.wait_send()
    send_in.wait_send()
    send_out.wait_send()
    each(XY, lambda k: copy_1(k).wait_send())
    each(XY, lambda k: copy_1s(k).wait_send())
    each(NR, lambda k: copy_2(k).wait_send())
    each(NR, lambda k: copy_3(k).wait_send())
    each(XY, lambda k: copy_4s(k).wait_send())
    each(NC, lambda k: copy_4(k).wait_send())
    save_mixed.wait()
    save_grad.wait()


def on_device(
    image, dw_kernel, dw_bias, layer_norm_gain, layer_norm_bias, w_in, b_in, w_out, b_out, cotangent
):
    vmem = pl.BlockSpec(memory_space=pltpu.VMEM)
    hbm = pl.BlockSpec(memory_space=pl.ANY)
    sem = pltpu.SemaphoreType.DMA
    scratch = [
        pltpu.VMEM((RH, CW, C), BF16),
        pltpu.VMEM((RH, CW, C), BF16),
        pltpu.VMEM((RH + 6, CW + 16, C), F32),
        pltpu.VMEM((RH + 6, CW + 16, C), F32),
        pltpu.VMEM((RH, CW, C), F32),
        pltpu.VMEM((56, 8, C), F32),
        pltpu.VMEM((C, HID), BF16),
        pltpu.VMEM((HID, C), BF16),
        pltpu.VMEM((RH, CW, C), BF16),
        pltpu.VMEM((RH, CW, C), BF16),
        pltpu.VMEM((RH, CW, C), BF16),
        pltpu.VMEM((C, HID), F32),
        pltpu.VMEM((C, HID), F32),
        pltpu.VMEM((8, HID), F32),
        pltpu.VMEM((8, C), F32),
        pltpu.VMEM((448, C), F32),
    ]
    for _ in range(2):
        scratch += [
            pltpu.VMEM((2, 3, CW, C), BF16),
            pltpu.VMEM((2, RH, 16, C), BF16),
            pltpu.VMEM((4, 3, 16, C), BF16),
        ]
    scratch += [
        pltpu.VMEM((XY, NR, 4, C), F32),
        pltpu.VMEM((XY, NR, 4, C), F32),
        pltpu.VMEM((XY, 4, C), F32),
        pltpu.VMEM((XY, 4, C), F32),
        pltpu.VMEM((NR, 2, 4, C), F32),
        pltpu.VMEM((NR, 2, 4, C), F32),
        pltpu.VMEM((NC, NR, 4, C), F32),
        pltpu.VMEM((XY, 4, C), F32),
        sem((6,)), sem((2,)), sem((2,)), sem((8,)), sem((8,)), sem((8,)), sem((8,)),
    ] + [sem((16,)) for _ in range(12)]
    outs = pl.pallas_call(
        kernel,
        out_shape=(
            jax.ShapeDtypeStruct((RH, CW, C), BF16),
            jax.ShapeDtypeStruct((RH, CW, C), BF16),
            jax.ShapeDtypeStruct((C // 2, HID), F32),
            jax.ShapeDtypeStruct((HID // 2, C), F32),
            jax.ShapeDtypeStruct((1, HID), F32),
            jax.ShapeDtypeStruct((7, 7, C), F32),
            jax.ShapeDtypeStruct((1, C), F32),
        ),
        in_specs=[hbm, vmem, vmem, vmem, vmem, hbm, vmem, hbm, vmem, hbm],
        out_specs=(hbm, hbm, vmem, vmem, vmem, vmem, vmem),
        scratch_shapes=scratch,
        compiler_params=pltpu.CompilerParams(
            collective_id=0, has_side_effects=True, vmem_limit_bytes=48 * 1024 * 1024
        ),
        name="convnext_block",
    )(
        image[0], dw_kernel, dw_bias.reshape(1, C), layer_norm_gain.reshape(1, C), layer_norm_bias.reshape(1, C),
        w_in, b_in.reshape(1, HID), w_out, b_out.reshape(1, C), cotangent[0],
    )
    mixed, d_image, g_in, g_out, g_b, g_k, g_gain = outs
    return (mixed[None], d_image[None], g_in, g_out, g_b.reshape(HID), g_k, g_gain.reshape(C))


def solution(mesh):
    return jax.shard_map(
        on_device,
        mesh=mesh,
        in_specs=(
            P("fsdp", "rows", "cols", None),
            P(),
            P(),
            P(),
            P(),
            P("fsdp", None),
            P(),
            P("fsdp", None),
            P(),
            P("fsdp", "rows", "cols", None),
        ),
        out_specs=(
            P("fsdp", "rows", "cols", None),
            P("fsdp", "rows", "cols", None),
            P("fsdp", None),
            P("fsdp", None),
            P(),
            P(),
            P(),
        ),
        check_vma=False,
    )
```

```python
import functools
import math

import jax
import jax.numpy as jnp
from jax import lax
from jax.experimental import pallas as pl
from jax.experimental.pallas import tpu as pltpu
from jax.sharding import PartitionSpec as P

MESH = pl.DeviceIdType.MESH
F32 = jnp.float32
BF16 = jnp.bfloat16

norm_eps = 1e-06
gelu_coef = math.sqrt(2.0 / math.pi)
cubic_coef = 0.044715

RH = 16
CW = 128
C = 128
HID = 512
XY = 16
NR = 16
NC = 8
BLOCK = 256
NBLOCKS = RH * CW // BLOCK

NT = (((1,), (1,)), ((), ()))
TN = (((0,), (0,)), ((), ()))


def tap_sums(source, first, rows, taps, acc, kb, flip):
    for b in range(7):
        weights = [kb[(6 - a) * 8 + (6 - b) if flip else a * 8 + b] for a in range(7)]
        for row in rows:
            value = source[row, pl.ds(first + 5 + b, 8), :]
            for h, a in taps(row):
                acc[h] = acc[h] + value * weights[a]
    return acc


def taps_all(row):
    return [(row - a, a) for a in range(7) if 0 <= row - a < RH]


def kernel(
    image, dw_kernel_in, dw_bias_in, gain_in, bias_in, w_in, b_in_in, w_out, b_out_in, cotangent,
    mixed_out, d_image_out, g_in_out, g_out_out, g_b_out, g_k_out, g_gain_out,
    mixed, dimg, g_out, g_b, g_k, g_gain, img, cot, dw_kernel, dw_bias, gain, bias, b_in, b_out, xp, dp, cv, kb, win, wout, dcb,
    gwi, gwo, bacc, gacc, kacc,
    hx_row, hx_col, hx_cor, hd_row, hd_col, hd_cor,
    grads, from_core, pair, r1, r2, a4, small, r1s, r2s, sa,
    local_sem, w_send, w_recv, hx_send, hx_recv, hd_send, hd_recv, x_send, x_recv, out_sem,
):
    mf = lax.axis_index("fsdp")
    mr = lax.axis_index("rows")
    mc = lax.axis_index("cols")
    me = mf * NC + mc
    core = mr % 2
    other = mr + 1 - 2 * core
    mz = mr // 2

    def xy_id(peer):
        return (peer // NC, mr, peer % NC)

    def row_id(peer):
        return (mf, peer, mc)

    up, down = (mr + NR - 1) % NR, (mr + 1) % NR
    left, right = (mc + NC - 1) % NC, (mc + 1) % NC

    loads = [
        (image, img), (cotangent, cot), (dw_kernel_in, dw_kernel), (dw_bias_in, dw_bias), (gain_in, gain), (bias_in, bias),
        (b_in_in, b_in), (b_out_in, b_out), (w_in, win.at[pl.ds(mf * 64, 64)]), (w_out, wout.at[pl.ds(mf * 256, 256)]),
    ]
    loads = [pltpu.make_async_copy(src, dst, local_sem.at[i]) for i, (src, dst) in enumerate(loads)]
    for i in (2, 3, 0, 1, 4, 5, 6, 7, 8, 9):
        loads[i].start()

    barrier = pltpu.get_barrier_semaphore()

    def greet(device):
        pl.semaphore_signal(barrier, inc=1, device_id=device, device_id_type=MESH)

    def greet_xy(k, _):
        greet(xy_id((me + k) % XY))
        return 0

    def greet_rows(k, _):
        greet(row_id((mr + k) % NR))
        return 0

    def greet_other(k, _):
        greet((mf, other, (mc + k) % NC))
        return 0

    beyond = (mr + NR - 1 + 2 * core) % NR
    greet((mf, beyond, left))
    greet((mf, beyond, right))
    lax.fori_loop(1, NC, greet_other, 0)
    lax.fori_loop(1, XY, greet_xy, 0)
    lax.fori_loop(1, NR, greet_rows, 0)

    loads[2].wait()
    loads[3].wait()
    for a in range(7):
        for b in range(7):
            kb[a * 8 + b] = jnp.broadcast_to(dw_kernel[a, pl.ds(b, 1), :], (8, C))
    conv_bias = jnp.broadcast_to(dw_bias[...], (8, C))

    loads[0].wait()

    def widen(r, _):
        xp[3 + r, pl.ds(8, CW), :] = img[r].astype(F32)
        return 0

    lax.fori_loop(0, RH, widen, 0)

    own_rows = range(3, RH + 3)
    edge_rows = (0, 1, 2, RH + 3, RH + 4, RH + 5)

    def conv_inner(wb, _):
        first = pl.multiple_of(wb * 8, 8)
        acc = tap_sums(xp, first, own_rows, taps_all, [conv_bias] * RH, kb, False)
        for h in range(RH):
            cv[h, pl.ds(first, 8), :] = acc[h]
        return 0

    lax.fori_loop(1, 4, conv_inner, 0)
    pl.semaphore_wait(barrier, 2 + NC - 1 + XY - 1 + NR - 1)

    def halo(source, rows_buf, col_buf, cor_buf, send, recv):
        plan = [
            (source.at[pl.ds(RH - 3, 3)], rows_buf.at[0], (mf, down, mc)),
            (source.at[pl.ds(0, 3)], rows_buf.at[1], (mf, up, mc)),
            (source.at[:, pl.ds(CW - 16, 16)], col_buf.at[0], (mf, mr, right)),
            (source.at[:, pl.ds(0, 16)], col_buf.at[1], (mf, mr, left)),
            (source.at[pl.ds(RH - 3, 3), pl.ds(CW - 16, 16)], cor_buf.at[0], (mf, down, right)),
            (source.at[pl.ds(RH - 3, 3), pl.ds(0, 16)], cor_buf.at[1], (mf, down, left)),
            (source.at[pl.ds(0, 3), pl.ds(CW - 16, 16)], cor_buf.at[2], (mf, up, right)),
            (source.at[pl.ds(0, 3), pl.ds(0, 16)], cor_buf.at[3], (mf, up, left)),
        ]
        copies = []
        for i, (src, dst, target) in enumerate(plan):
            copy = pltpu.make_async_remote_copy(
                src_ref=src, dst_ref=dst, send_sem=send.at[i], recv_sem=recv.at[i], device_id=target, device_id_type=MESH
            )
            copy.start()
            copies.append(copy)
        return copies

    has_up = jnp.where(mr > 0, 1.0, 0.0).astype(F32)
    has_down = jnp.where(mr < NR - 1, 1.0, 0.0).astype(F32)
    has_left = jnp.where(mc > 0, 1.0, 0.0).astype(F32)
    has_right = jnp.where(mc < NC - 1, 1.0, 0.0).astype(F32)

    def unpack_halo(padded, rows_buf, col_buf, cor_buf):
        for i in range(3):
            padded[i, pl.ds(8, CW), :] = rows_buf[0, i].astype(F32) * has_up
            padded[RH + 3 + i, pl.ds(8, CW), :] = rows_buf[1, i].astype(F32) * has_down
            padded[i, pl.ds(0, 8), :] = cor_buf[0, i].astype(F32)[8:16] * (has_up * has_left)
            padded[i, pl.ds(CW + 8, 8), :] = cor_buf[1, i].astype(F32)[0:8] * (has_up * has_right)
            padded[RH + 3 + i, pl.ds(0, 8), :] = cor_buf[2, i].astype(F32)[8:16] * (has_down * has_left)
            padded[RH + 3 + i, pl.ds(CW + 8, 8), :] = cor_buf[3, i].astype(F32)[0:8] * (has_down * has_right)

        def side(r, _):
            padded[3 + r, pl.ds(0, 8), :] = col_buf[0, r].astype(F32)[8:16] * has_left
            padded[3 + r, pl.ds(CW + 8, 8), :] = col_buf[1, r].astype(F32)[0:8] * has_right
            return 0

        lax.fori_loop(0, RH, side, 0)

    hx = halo(image, hx_row, hx_col, hx_cor, hx_send, hx_recv)
    partner = (1 - mf, mr, mc)
    send_in = pltpu.make_async_remote_copy(
        src_ref=w_in, dst_ref=win.at[pl.ds(mf * 64, 64)], send_sem=w_send.at[0], recv_sem=w_recv.at[0],
        device_id=partner, device_id_type=MESH,
    )
    send_in.start()
    send_out = pltpu.make_async_remote_copy(
        src_ref=w_out, dst_ref=wout.at[pl.ds(mf * 256, 256)], send_sem=w_send.at[1], recv_sem=w_recv.at[1],
        device_id=partner, device_id_type=MESH,
    )
    send_out.start()

    lax.fori_loop(4, CW // 8 - 1, conv_inner, 0)

    for copy in hx:
        copy.wait_recv()
    unpack_halo(xp, hx_row, hx_col, hx_cor)

    def conv_edge(wb, _):
        first = pl.multiple_of(wb * 8, 8)
        acc = [None] * RH
        touched = (0, 1, 2, RH - 3, RH - 2, RH - 1)
        for h in touched:
            acc[h] = cv[h, pl.ds(first, 8), :]
        acc = tap_sums(xp, first, edge_rows, taps_all, acc, kb, False)
        for h in touched:
            cv[h, pl.ds(first, 8), :] = acc[h]
        return 0

    lax.fori_loop(1, CW // 8 - 1, conv_edge, 0)

    def conv_side(i, _):
        first = pl.multiple_of(i * (CW - 8), 8)
        acc = tap_sums(xp, first, range(RH + 6), taps_all, [conv_bias] * RH, kb, False)
        for h in range(RH):
            cv[h, pl.ds(first, 8), :] = acc[h]
        return 0

    lax.fori_loop(0, 2, conv_side, 0)

    for i in (1, 4, 5, 6, 7, 8, 9):
        loads[i].wait()
    send_in.wait_recv()
    send_out.wait_recv()
    gwi[...] = jnp.zeros_like(gwi)
    gwo[...] = jnp.zeros_like(gwo)
    bacc[...] = jnp.zeros_like(bacc)
    gacc[...] = jnp.zeros_like(gacc)
    rows_per = BLOCK // CW

    def pointwise(i, _):
        r0 = i * rows_per
        conv = cv[pl.ds(r0, rows_per)].reshape(BLOCK, C)
        center = jnp.mean(conv, axis=-1, keepdims=True)
        spread = conv - center
        rstd = lax.rsqrt(jnp.mean(spread * spread, axis=-1, keepdims=True) + norm_eps)
        xhat = spread * rstd
        normed = (xhat * gain[...] + bias[...]).astype(BF16)
        up_b = cot[pl.ds(r0, rows_per)].reshape(BLOCK, C)
        out_sum = jnp.zeros((BLOCK, C), F32)
        dn = jnp.zeros((BLOCK, C), F32)
        half = HID // 2
        for j in range(2):
            cols = slice(j * half, (j + 1) * half)
            pre = jnp.dot(normed, win[:, cols], preferred_element_type=F32) + b_in[:, cols]
            square = pre * pre
            tanh_val = jnp.tanh(pre * (gelu_coef + (gelu_coef * cubic_coef) * square))
            half_gate = 0.5 + 0.5 * tanh_val
            hidden = (pre * half_gate).astype(BF16)
            slope = half_gate + (pre * (0.5 - 0.5 * tanh_val * tanh_val)) * (
                gelu_coef + (3.0 * gelu_coef * cubic_coef) * square
            )
            d_hidden = lax.dot_general(up_b, wout[cols, :], NT, preferred_element_type=F32)
            d_wide = d_hidden * slope
            d_pre = d_wide.astype(BF16)
            bacc[:, cols] += jnp.sum(d_wide.reshape(BLOCK // 8, 8, half), axis=0)
            out_sum = out_sum + jnp.dot(hidden, wout[cols, :], preferred_element_type=F32)
            dn = dn + lax.dot_general(d_pre, win[:, cols], NT, preferred_element_type=F32)
            gwi[:, cols] += lax.dot_general(normed, d_pre, TN, preferred_element_type=F32)
            gwo[:, cols] += lax.dot_general(up_b, hidden, TN, preferred_element_type=F32)
        field = img[pl.ds(r0, rows_per)].reshape(BLOCK, C).astype(F32)
        mixed[pl.ds(r0, rows_per)] = (field + out_sum + b_out[...]).astype(BF16).reshape(rows_per, CW, C)
        gacc[...] += jnp.sum((dn * xhat).reshape(BLOCK // 8, 8, C), axis=0)
        q = dn * gain[...]
        d_conv = (
            rstd * (q - jnp.mean(q, axis=-1, keepdims=True) - xhat * jnp.mean(q * xhat, axis=-1, keepdims=True))
        ).astype(BF16)
        d_rows = d_conv.reshape(rows_per, CW, C)
        dcb[pl.ds(r0, rows_per)] = d_rows
        dp[pl.ds(3 + r0, rows_per), pl.ds(8, CW), :] = d_rows.astype(F32)
        return 0

    lax.fori_loop(0, NBLOCKS, pointwise, 0)

    hd = halo(dcb, hd_row, hd_col, hd_cor, hd_send, hd_recv)
    saves = []

    def save_part(src, dst):
        copy = pltpu.make_async_copy(src, dst, out_sem.at[len(saves)])
        copy.start()
        saves.append(copy)

    save_part(mixed, mixed_out)

    for q in range(4):
        turned = gwo[:, q * 128 : (q + 1) * 128].T
        for u in range(16):
            p, at = q * 4 + u // 4, u % 4
            grads[1, p * 8 : (p + 1) * 8, at * 128 : (at + 1) * 128] = turned[u * 8 : (u + 1) * 8]
    grads[0] = gwi[...]

    def remote(src, dst, sem, device):
        return pltpu.make_async_remote_copy(
            src_ref=src, dst_ref=dst, send_sem=x_send.at[sem], recv_sem=x_recv.at[sem], device_id=device, device_id_type=MESH
        )

    def start(copies):
        for copy in copies:
            copy.start()

    def arrived(ref, sem):
        pltpu.make_async_copy(ref, ref, x_recv.at[sem]).wait()

    def left_here(ref, sem):
        pltpu.make_async_copy(ref, ref, x_send.at[sem]).wait()

    far_xy = (10, 6, 2, 14, 8, 9, 11, 7, 12, 4, 5, 13, 3, 1, 15)
    far_z = (4, 3, 5, 2, 6, 1, 7)
    far_rows = (8, 7, 9, 6, 10, 5, 11, 4, 12, 3, 13, 2, 14, 1, 15)
    far_cols = (6, 2, 4, 5, 7, 3, 1)

    start([remote(grads.at[1 - core], from_core, 0, (mf, other, mc))])

    def send_pair():
        arrived(from_core, 0)

        def add(p, _):
            rows = pl.ds(pl.multiple_of(p * 8, 8), 8)
            pair[rows, :] = grads[core, rows, :] + from_core[rows, :]
            return 0

        lax.fori_loop(0, XY, add, 0)
        copies = []
        for k in far_xy:
            peer = (me + k) % XY
            rows = pl.ds(pl.multiple_of(peer * 8, 8), 8)
            copies.append(remote(pair.at[rows], r1.at[k - 1], 1, xy_id(peer)))
        start(copies)

    def send_sums():
        arrived(r1, 1)
        total = pair[pl.ds(pl.multiple_of(me * 8, 8), 8), :]
        for k in range(XY - 1):
            total = total + r1[k]
        r2[mz] = total
        start([remote(r2.at[mz], r2.at[mz], 2, row_id((mr + 2 * k) % NR)) for k in far_z])

    def send_result():
        arrived(r2.at[pl.ds(0, NR // 2 - 1)], 2)
        total = r2[0]
        for z in range(1, NR // 2):
            total = total + r2[z]
        a4[core, mc] = total
        copies = []
        for k in far_cols:
            for row in (other, mr):
                copies.append(remote(a4.at[core, mc], a4.at[core, mc], 3, (mf, row, (mc + k) % NC)))
        copies.append(remote(a4.at[core, mc], a4.at[core, mc], 3, (mf, other, mc)))
        start(copies)

    def send_small():
        start([remote(small.at[(me + k) % XY], r1s.at[k - 1], 4, xy_id((me + k) % XY)) for k in far_xy])

    def send_small_sums():
        arrived(r1s, 4)
        total = small[me]
        for k in range(XY - 1):
            total = total + r1s[k]
        r2s[mr] = total
        start([remote(r2s.at[mr], r2s.at[mr], 5, row_id((mr + k) % NR)) for k in far_rows])

    def send_small_result():
        arrived(r2s.at[pl.ds(0, NR - 1)], 5)
        total = r2s[0]
        for r in range(1, NR):
            total = total + r2s[r]
        sa[me] = total
        start([remote(sa.at[me], sa.at[me], 6, xy_id((me + k) % XY)) for k in far_xy])

    def tap_gradient(b):
        def step(wb, acc):
            first = pl.multiple_of(wb * 8, 8)
            acc = list(acc)
            grad = [dp[3 + h, pl.ds(first + 8, 8), :] for h in range(RH)]
            for row in range(RH + 6):
                value = xp[row, pl.ds(first + 5 + b, 8), :]
                for h, a in taps_all(row):
                    acc[a] = acc[a] + value * grad[h]
            return tuple(acc)

        acc = lax.fori_loop(0, CW // 8, step, tuple(jnp.zeros((8, C), F32) for _ in range(7)))
        for a in range(7):
            kacc[pl.ds((a * 8 + b) * 8, 8), :] = acc[a]

    for b in range(7):
        if b == 3:
            send_pair()
        tap_gradient(b)
    for a in range(7):
        kacc[pl.ds((a * 8 + 7) * 8, 8), :] = jnp.zeros((8, C), F32)
    for a in range(7):
        total = kacc[pl.ds(a * 64, 8, stride=8), :]
        for s in range(1, 8):
            total = total + kacc[pl.ds(a * 64 + s, 8, stride=8), :]
        small[2 * a] = total[0:4]
        small[2 * a + 1] = total[4:8]
    for q in range(4):
        small[14, pl.ds(q, 1), :] = jnp.sum(bacc[:, q * 128 : (q + 1) * 128], axis=0, keepdims=True)
    small[15] = jnp.broadcast_to(jnp.sum(gacc[...], axis=0, keepdims=True), (4, C))
    send_small()

    for copy in hd:
        copy.wait_recv()
    unpack_halo(dp, hd_row, hd_col, hd_cor)

    def image_gradient(wb, _):
        first = pl.multiple_of(wb * 8, 8)
        acc = tap_sums(dp, first, range(RH + 6), taps_all, [jnp.zeros((8, C), F32)] * RH, kb, True)
        for h in range(RH):
            cv[h, pl.ds(first, 8), :] = acc[h]
        return 0

    def finish(wb, _):
        first = pl.multiple_of(wb * 16, 16)
        columns = pl.ds(first, 16)
        for h in range(RH):
            dimg[h, columns, :] = (cot[h, columns, :].astype(F32) + cv[h, columns, :]).astype(BF16)
        return 0

    lax.fori_loop(0, 6, image_gradient, 0)
    send_sums()
    lax.fori_loop(6, 12, image_gradient, 0)
    send_small_sums()
    lax.fori_loop(12, 16, image_gradient, 0)
    lax.fori_loop(0, 8, finish, 0)
    save_part(dimg, d_image_out)
    send_result()
    send_small_result()

    arrived(r1, 3)
    for j in range(NC):
        save_part(a4.at[0, j], g_in_out.at[pl.ds(j * 8, 8)])

    def place(j, _):
        for q in range(4):
            at = pl.multiple_of(j * 32 + q * 8, 8)
            g_out[pl.ds(at, 8), :] = a4[1, j, :, q * 128 : (q + 1) * 128]
        return 0

    lax.fori_loop(0, NC, place, 0)
    save_part(g_out, g_out_out)
    arrived(sa.at[pl.ds(0, XY - 1)], 6)
    for a in range(7):
        g_k[a, pl.ds(0, 4), :] = sa[2 * a]
        g_k[a, pl.ds(4, 3), :] = sa[2 * a + 1][0:3]
    for q in range(4):
        g_b[:, q * 128 : (q + 1) * 128] = sa[14, pl.ds(q, 1), :]
    g_gain[...] = sa[15, pl.ds(0, 1), :]
    save_part(g_k, g_k_out)
    save_part(g_b, g_b_out)
    save_part(g_gain, g_gain_out)

    for copy in hx:
        copy.wait_send()
    for copy in hd:
        copy.wait_send()
    send_in.wait_send()
    send_out.wait_send()
    left_here(from_core, 0)
    left_here(r1, 1)
    left_here(r2.at[pl.ds(0, NR // 2 - 1)], 2)
    left_here(r1, 3)
    left_here(r1s, 4)
    left_here(r2s.at[pl.ds(0, NR - 1)], 5)
    left_here(sa.at[pl.ds(0, XY - 1)], 6)
    for copy in saves:
        copy.wait()


def save(*refs):
    sources, targets, sem = refs[:7], refs[7:14], refs[14]
    copies = [pltpu.make_async_copy(src, dst, sem.at[i]) for i, (src, dst) in enumerate(zip(sources, targets))]
    for copy in copies:
        copy.start()
    for copy in copies:
        copy.wait()


def on_device(
    image, dw_kernel, dw_bias, layer_norm_gain, layer_norm_bias, w_in, b_in, w_out, b_out, cotangent
):
    hbm = pl.BlockSpec(memory_space=pltpu.HBM)
    sem = pltpu.SemaphoreType.DMA
    scratch = [
        pltpu.VMEM((RH, CW, C), BF16),
        pltpu.VMEM((RH, CW, C), BF16),
        pltpu.VMEM((HID // 2, C), F32),
        pltpu.VMEM((1, HID), F32),
        pltpu.VMEM((7, 7, C), F32),
        pltpu.VMEM((1, C), F32),
        pltpu.VMEM((RH, CW, C), BF16),
        pltpu.VMEM((RH, CW, C), BF16),
        pltpu.VMEM((7, 7, C), F32),
        pltpu.VMEM((1, C), F32),
        pltpu.VMEM((1, C), F32),
        pltpu.VMEM((1, C), F32),
        pltpu.VMEM((1, HID), F32),
        pltpu.VMEM((1, C), F32),
        pltpu.VMEM((RH + 6, CW + 16, C), F32),
        pltpu.VMEM((RH + 6, CW + 16, C), F32),
        pltpu.VMEM((RH, CW, C), F32),
        pltpu.VMEM((56, 8, C), F32),
        pltpu.VMEM((C, HID), BF16),
        pltpu.VMEM((HID, C), BF16),
        pltpu.VMEM((RH, CW, C), BF16),
        pltpu.VMEM((C, HID), F32),
        pltpu.VMEM((C, HID), F32),
        pltpu.VMEM((8, HID), F32),
        pltpu.VMEM((8, C), F32),
        pltpu.VMEM((448, C), F32),
    ]
    for _ in range(2):
        scratch += [
            pltpu.VMEM((2, 3, CW, C), BF16),
            pltpu.VMEM((2, RH, 16, C), BF16),
            pltpu.VMEM((4, 3, 16, C), BF16),
        ]
    scratch += [
        pltpu.VMEM((2, C, HID), F32),
        pltpu.VMEM((C, HID), F32),
        pltpu.VMEM((C, HID), F32),
        pltpu.VMEM((XY - 1, 8, HID), F32),
        pltpu.VMEM((NR // 2, 8, HID), F32),
        pltpu.VMEM((2, NC, 8, HID), F32),
        pltpu.VMEM((XY, 4, C), F32),
        pltpu.VMEM((XY - 1, 4, C), F32),
        pltpu.VMEM((NR, 4, C), F32),
        pltpu.VMEM((XY, 4, C), F32),
        sem((10,)), sem((2,)), sem((2,)), sem((8,)), sem((8,)), sem((8,)), sem((8,)), sem((7,)), sem((7,)), sem((14,)),
    ]
    shapes = (
        jax.ShapeDtypeStruct((RH, CW, C), BF16),
        jax.ShapeDtypeStruct((RH, CW, C), BF16),
        jax.ShapeDtypeStruct((C // 2, HID), F32),
        jax.ShapeDtypeStruct((HID // 2, C), F32),
        jax.ShapeDtypeStruct((1, HID), F32),
        jax.ShapeDtypeStruct((7, 7, C), F32),
        jax.ShapeDtypeStruct((1, C), F32),
    )
    outs = pl.pallas_call(
        kernel,
        out_shape=shapes,
        in_specs=[hbm] * 10,
        out_specs=(hbm,) * 7,
        scratch_shapes=scratch,
        compiler_params=pltpu.CompilerParams(
            collective_id=0, has_side_effects=True, vmem_limit_bytes=63 * 1024 * 1024
        ),
        name="convnext_block",
    )(
        image[0], dw_kernel, dw_bias.reshape(1, C), layer_norm_gain.reshape(1, C), layer_norm_bias.reshape(1, C),
        w_in, b_in.reshape(1, HID), w_out, b_out.reshape(1, C), cotangent[0],
    )
    outs = pl.pallas_call(
        save,
        out_shape=shapes,
        in_specs=[pl.BlockSpec(memory_space=pl.ANY)] * 7,
        out_specs=(hbm,) * 7,
        scratch_shapes=[sem((7,))],
        compiler_params=pltpu.CompilerParams(vmem_limit_bytes=63 * 1024 * 1024),
        name="save_outputs",
    )(*outs)
    mixed, d_image, g_in, g_out, g_b, g_k, g_gain = outs
    return (mixed[None], d_image[None], g_in, g_out, g_b.reshape(HID), g_k, g_gain.reshape(C))


def solution(mesh):
    return jax.shard_map(
        on_device,
        mesh=mesh,
        in_specs=(
            P("fsdp", "rows", "cols", None),
            P(),
            P(),
            P(),
            P(),
            P("fsdp", None),
            P(),
            P("fsdp", None),
            P(),
            P("fsdp", "rows", "cols", None),
        ),
        out_specs=(
            P("fsdp", "rows", "cols", None),
            P("fsdp", "rows", "cols", None),
            P("fsdp", None),
            P("fsdp", None),
            P(),
            P(),
            P(),
        ),
        check_vma=False,
    )
```

```python
import functools
import math

import jax
import jax.numpy as jnp
from jax import lax
from jax.experimental import pallas as pl
from jax.experimental.pallas import tpu as pltpu
from jax.sharding import PartitionSpec as P

MESH = pl.DeviceIdType.MESH
F32 = jnp.float32
BF16 = jnp.bfloat16

norm_eps = 1e-06
gelu_coef = math.sqrt(2.0 / math.pi)
cubic_coef = 0.044715

RH = 16
CW = 128
C = 128
HID = 512
XY = 16
NR = 16
NC = 8
PIX = RH * CW

NT = (((1,), (1,)), ((), ()))
TN = (((0,), (0,)), ((), ()))


def tap_sums(source, first, rows, taps, acc, kb, flip):
    for b in range(7):
        weights = [kb[(6 - a) * 8 + (6 - b) if flip else a * 8 + b] for a in range(7)]
        for row in rows:
            value = source[row, pl.ds(first + 5 + b, 8), :]
            for h, a in taps(row):
                acc[h] = acc[h] + value * weights[a]
    return acc


def taps_all(row):
    return [(row - a, a) for a in range(7) if 0 <= row - a < RH]


def kernel(
    image, dw_kernel_in, dw_bias_in, gain_in, bias_in, w_in, b_in_in, w_out, b_out_in, cotangent,
    mixed_out, d_image_out, g_in_out, g_out_out, g_b_out, g_k_out, g_gain_out,
    mixed, dimg, g_out, g_b, g_k, g_gain, img, cot, dw_kernel, dw_bias, gain, bias, b_in, b_out, xp, dp, cv, kb, win, wout, dcb,
    bacc, gacc, kacc,
    hx_row, hx_col, hx_cor, hd_row, hd_col, hd_cor,
    grads, from_core, pair, r1, r2, a4, small, r1s, r2s, sa,
    local_sem, w_send, w_recv, hx_send, hx_recv, hd_send, hd_recv, x_send, x_recv, out_sem,
):
    mf = lax.axis_index("fsdp")
    mr = lax.axis_index("rows")
    mc = lax.axis_index("cols")
    me = mf * NC + mc
    core = mr % 2
    other = mr + 1 - 2 * core
    mz = mr // 2

    def xy_id(peer):
        return (peer // NC, mr, peer % NC)

    def row_id(peer):
        return (mf, peer, mc)

    up, down = (mr + NR - 1) % NR, (mr + 1) % NR
    left, right = (mc + NC - 1) % NC, (mc + 1) % NC

    loads = [
        (image, img), (cotangent, cot), (dw_kernel_in, dw_kernel), (dw_bias_in, dw_bias), (gain_in, gain), (bias_in, bias),
        (b_in_in, b_in), (b_out_in, b_out), (w_in, win.at[pl.ds(mf * 64, 64)]), (w_out, wout.at[pl.ds(mf * 256, 256)]),
    ]
    loads = [pltpu.make_async_copy(src, dst, local_sem.at[i]) for i, (src, dst) in enumerate(loads)]
    for i in (2, 3, 0, 1, 4, 5, 6, 7, 8, 9):
        loads[i].start()

    barrier = pltpu.get_barrier_semaphore()

    def greet(device):
        pl.semaphore_signal(barrier, inc=1, device_id=device, device_id_type=MESH)

    def greet_xy(k, _):
        greet(xy_id((me + k) % XY))
        return 0

    def greet_rows(k, _):
        greet(row_id((mr + k) % NR))
        return 0

    def greet_other(k, _):
        greet((mf, other, (mc + k) % NC))
        return 0

    beyond = (mr + NR - 1 + 2 * core) % NR
    greet((mf, beyond, left))
    greet((mf, beyond, right))
    lax.fori_loop(1, NC, greet_other, 0)
    lax.fori_loop(1, XY, greet_xy, 0)
    lax.fori_loop(1, NR, greet_rows, 0)

    loads[2].wait()
    loads[3].wait()
    for a in range(7):
        for b in range(7):
            kb[a * 8 + b] = jnp.broadcast_to(dw_kernel[a, pl.ds(b, 1), :], (8, C))
    conv_bias = jnp.broadcast_to(dw_bias[...], (8, C))

    loads[0].wait()

    def widen(r, _):
        xp[3 + r, pl.ds(8, CW), :] = img[r].astype(F32)
        return 0

    lax.fori_loop(0, RH, widen, 0)

    own_rows = range(3, RH + 3)
    edge_rows = (0, 1, 2, RH + 3, RH + 4, RH + 5)

    def conv_inner(wb, _):
        first = pl.multiple_of(wb * 8, 8)
        acc = tap_sums(xp, first, own_rows, taps_all, [conv_bias] * RH, kb, False)
        for h in range(RH):
            cv[h, pl.ds(first, 8), :] = acc[h]
        return 0

    lax.fori_loop(1, 4, conv_inner, 0)
    pl.semaphore_wait(barrier, 2 + NC - 1 + XY - 1 + NR - 1)

    def halo(source, rows_buf, col_buf, cor_buf, send, recv):
        plan = [
            (source.at[pl.ds(RH - 3, 3)], rows_buf.at[0], (mf, down, mc)),
            (source.at[pl.ds(0, 3)], rows_buf.at[1], (mf, up, mc)),
            (source.at[:, pl.ds(CW - 16, 16)], col_buf.at[0], (mf, mr, right)),
            (source.at[:, pl.ds(0, 16)], col_buf.at[1], (mf, mr, left)),
            (source.at[pl.ds(RH - 3, 3), pl.ds(CW - 16, 16)], cor_buf.at[0], (mf, down, right)),
            (source.at[pl.ds(RH - 3, 3), pl.ds(0, 16)], cor_buf.at[1], (mf, down, left)),
            (source.at[pl.ds(0, 3), pl.ds(CW - 16, 16)], cor_buf.at[2], (mf, up, right)),
            (source.at[pl.ds(0, 3), pl.ds(0, 16)], cor_buf.at[3], (mf, up, left)),
        ]
        copies = []
        for i, (src, dst, target) in enumerate(plan):
            copy = pltpu.make_async_remote_copy(
                src_ref=src, dst_ref=dst, send_sem=send.at[i], recv_sem=recv.at[i], device_id=target, device_id_type=MESH
            )
            copy.start()
            copies.append(copy)
        return copies

    has_up = jnp.where(mr > 0, 1.0, 0.0).astype(F32)
    has_down = jnp.where(mr < NR - 1, 1.0, 0.0).astype(F32)
    has_left = jnp.where(mc > 0, 1.0, 0.0).astype(F32)
    has_right = jnp.where(mc < NC - 1, 1.0, 0.0).astype(F32)

    def unpack_halo(padded, rows_buf, col_buf, cor_buf):
        for i in range(3):
            padded[i, pl.ds(8, CW), :] = rows_buf[0, i].astype(F32) * has_up
            padded[RH + 3 + i, pl.ds(8, CW), :] = rows_buf[1, i].astype(F32) * has_down
            padded[i, pl.ds(0, 8), :] = cor_buf[0, i].astype(F32)[8:16] * (has_up * has_left)
            padded[i, pl.ds(CW + 8, 8), :] = cor_buf[1, i].astype(F32)[0:8] * (has_up * has_right)
            padded[RH + 3 + i, pl.ds(0, 8), :] = cor_buf[2, i].astype(F32)[8:16] * (has_down * has_left)
            padded[RH + 3 + i, pl.ds(CW + 8, 8), :] = cor_buf[3, i].astype(F32)[0:8] * (has_down * has_right)

        def side(r, _):
            padded[3 + r, pl.ds(0, 8), :] = col_buf[0, r].astype(F32)[8:16] * has_left
            padded[3 + r, pl.ds(CW + 8, 8), :] = col_buf[1, r].astype(F32)[0:8] * has_right
            return 0

        lax.fori_loop(0, RH, side, 0)

    hx = halo(image, hx_row, hx_col, hx_cor, hx_send, hx_recv)
    partner = (1 - mf, mr, mc)
    send_in = pltpu.make_async_remote_copy(
        src_ref=w_in, dst_ref=win.at[pl.ds(mf * 64, 64)], send_sem=w_send.at[0], recv_sem=w_recv.at[0],
        device_id=partner, device_id_type=MESH,
    )
    send_in.start()
    send_out = pltpu.make_async_remote_copy(
        src_ref=w_out, dst_ref=wout.at[pl.ds(mf * 256, 256)], send_sem=w_send.at[1], recv_sem=w_recv.at[1],
        device_id=partner, device_id_type=MESH,
    )
    send_out.start()

    lax.fori_loop(4, CW // 8 - 1, conv_inner, 0)

    for copy in hx:
        copy.wait_recv()
    unpack_halo(xp, hx_row, hx_col, hx_cor)

    def conv_edge(wb, _):
        first = pl.multiple_of(wb * 8, 8)
        acc = [None] * RH
        touched = (0, 1, 2, RH - 3, RH - 2, RH - 1)
        for h in touched:
            acc[h] = cv[h, pl.ds(first, 8), :]
        acc = tap_sums(xp, first, edge_rows, taps_all, acc, kb, False)
        for h in touched:
            cv[h, pl.ds(first, 8), :] = acc[h]
        return 0

    lax.fori_loop(1, CW // 8 - 1, conv_edge, 0)

    def conv_side(i, _):
        first = pl.multiple_of(i * (CW - 8), 8)
        acc = tap_sums(xp, first, range(RH + 6), taps_all, [conv_bias] * RH, kb, False)
        for h in range(RH):
            cv[h, pl.ds(first, 8), :] = acc[h]
        return 0

    lax.fori_loop(0, 2, conv_side, 0)

    for i in (1, 4, 5, 6, 7, 8, 9):
        loads[i].wait()
    send_in.wait_recv()
    send_out.wait_recv()
    def remote(src, dst, sem, device):
        return pltpu.make_async_remote_copy(
            src_ref=src, dst_ref=dst, send_sem=x_send.at[sem], recv_sem=x_recv.at[sem], device_id=device, device_id_type=MESH
        )

    def start(copies):
        for copy in copies:
            copy.start()

    def arrived(ref, sem):
        pltpu.make_async_copy(ref, ref, x_recv.at[sem]).wait()

    def left_here(ref, sem):
        pltpu.make_async_copy(ref, ref, x_send.at[sem]).wait()

    far_xy = (10, 6, 2, 14, 8, 9, 11, 7, 12, 4, 5, 13, 3, 1, 15)
    far_z = (4, 3, 5, 2, 6, 1, 7)
    far_rows = (8, 7, 9, 6, 10, 5, 11, 4, 12, 3, 13, 2, 14, 1, 15)
    far_cols = (6, 2, 4, 5, 7, 3, 1)

    conv = cv[...].reshape(PIX, C)
    center = jnp.mean(conv, axis=-1, keepdims=True)
    spread = conv - center
    rstd = lax.rsqrt(jnp.mean(spread * spread, axis=-1, keepdims=True) + norm_eps)
    xhat = spread * rstd
    normed = (xhat * gain[...] + bias[...]).astype(BF16)
    upstream = cot[...].reshape(PIX, C)
    pre = jnp.dot(normed, win[...], preferred_element_type=F32) + b_in[...]
    square = pre * pre
    tanh_val = jnp.tanh(pre * (gelu_coef + (gelu_coef * cubic_coef) * square))
    half_gate = 0.5 + 0.5 * tanh_val
    hidden = (pre * half_gate).astype(BF16)
    slope = half_gate + (pre * (0.5 - 0.5 * tanh_val * tanh_val)) * (
        gelu_coef + (3.0 * gelu_coef * cubic_coef) * square
    )
    d_wide = lax.dot_general(upstream, wout[...], NT, preferred_element_type=F32) * slope
    d_pre = d_wide.astype(BF16)
    bacc[...] = jnp.sum(d_wide.reshape(PIX // 8, 8, HID), axis=0)

    grads[0] = lax.dot_general(normed, d_pre, TN, preferred_element_type=F32)
    out_turned = lax.dot_general(upstream, hidden, TN, preferred_element_type=F32)
    for q in range(4):
        turned = out_turned[:, q * 128 : (q + 1) * 128].T
        for u in range(16):
            p, at = q * 4 + u // 4, u % 4
            grads[1, p * 8 : (p + 1) * 8, at * 128 : (at + 1) * 128] = turned[u * 8 : (u + 1) * 8]
    start([remote(grads.at[1 - core], from_core, 0, (mf, other, mc))])

    out_sum = jnp.dot(hidden, wout[...], preferred_element_type=F32)
    field = img[...].reshape(PIX, C).astype(F32)
    mixed[...] = (field + out_sum + b_out[...]).astype(BF16).reshape(RH, CW, C)
    dn = lax.dot_general(d_pre, win[...], NT, preferred_element_type=F32)
    gacc[...] = jnp.sum((dn * xhat).reshape(PIX // 8, 8, C), axis=0)
    q = dn * gain[...]
    d_conv = (
        rstd * (q - jnp.mean(q, axis=-1, keepdims=True) - xhat * jnp.mean(q * xhat, axis=-1, keepdims=True))
    ).astype(BF16)
    d_rows = d_conv.reshape(RH, CW, C)
    dcb[...] = d_rows
    dp[pl.ds(3, RH), pl.ds(8, CW), :] = d_rows.astype(F32)

    hd = halo(dcb, hd_row, hd_col, hd_cor, hd_send, hd_recv)
    saves = []

    def save_part(src, dst):
        copy = pltpu.make_async_copy(src, dst, out_sem.at[len(saves)])
        copy.start()
        saves.append(copy)

    save_part(mixed, mixed_out)

    def send_pair():
        arrived(from_core, 0)

        def add(p, _):
            rows = pl.ds(pl.multiple_of(p * 8, 8), 8)
            pair[rows, :] = grads[core, rows, :] + from_core[rows, :]
            return 0

        lax.fori_loop(0, XY, add, 0)
        copies = []
        for k in far_xy:
            peer = (me + k) % XY
            rows = pl.ds(pl.multiple_of(peer * 8, 8), 8)
            copies.append(remote(pair.at[rows], r1.at[k - 1], 1, xy_id(peer)))
        start(copies)

    def send_sums():
        arrived(r1, 1)
        total = pair[pl.ds(pl.multiple_of(me * 8, 8), 8), :]
        for k in range(XY - 1):
            total = total + r1[k]
        r2[mz] = total
        start([remote(r2.at[mz], r2.at[mz], 2, row_id((mr + 2 * k) % NR)) for k in far_z])

    def send_result():
        arrived(r2.at[pl.ds(0, NR // 2 - 1)], 2)
        total = r2[0]
        for z in range(1, NR // 2):
            total = total + r2[z]
        a4[core, mc] = total
        copies = []
        for k in far_cols:
            for row in (other, mr):
                copies.append(remote(a4.at[core, mc], a4.at[core, mc], 3, (mf, row, (mc + k) % NC)))
        copies.append(remote(a4.at[core, mc], a4.at[core, mc], 3, (mf, other, mc)))
        start(copies)

    def send_small():
        start([remote(small.at[(me + k) % XY], r1s.at[k - 1], 4, xy_id((me + k) % XY)) for k in far_xy])

    def send_small_sums():
        arrived(r1s, 4)
        total = small[me]
        for k in range(XY - 1):
            total = total + r1s[k]
        r2s[mr] = total
        start([remote(r2s.at[mr], r2s.at[mr], 5, row_id((mr + k) % NR)) for k in far_rows])

    def send_small_result():
        arrived(r2s.at[pl.ds(0, NR - 1)], 5)
        total = r2s[0]
        for r in range(1, NR):
            total = total + r2s[r]
        sa[me] = total
        start([remote(sa.at[me], sa.at[me], 6, xy_id((me + k) % XY)) for k in far_xy])

    def tap_gradient(b):
        def step(wb, acc):
            first = pl.multiple_of(wb * 8, 8)
            acc = list(acc)
            grad = [dp[3 + h, pl.ds(first + 8, 8), :] for h in range(RH)]
            for row in range(RH + 6):
                value = xp[row, pl.ds(first + 5 + b, 8), :]
                for h, a in taps_all(row):
                    acc[a] = acc[a] + value * grad[h]
            return tuple(acc)

        acc = lax.fori_loop(0, CW // 8, step, tuple(jnp.zeros((8, C), F32) for _ in range(7)), unroll=4)
        for a in range(7):
            kacc[pl.ds((a * 8 + b) * 8, 8), :] = acc[a]

    for b in range(7):
        if b == 3:
            send_pair()
        tap_gradient(b)
    for a in range(7):
        kacc[pl.ds((a * 8 + 7) * 8, 8), :] = jnp.zeros((8, C), F32)
    for a in range(7):
        total = kacc[pl.ds(a * 64, 8, stride=8), :]
        for s in range(1, 8):
            total = total + kacc[pl.ds(a * 64 + s, 8, stride=8), :]
        small[2 * a] = total[0:4]
        small[2 * a + 1] = total[4:8]
    for q in range(4):
        small[14, pl.ds(q, 1), :] = jnp.sum(bacc[:, q * 128 : (q + 1) * 128], axis=0, keepdims=True)
    small[15] = jnp.broadcast_to(jnp.sum(gacc[...], axis=0, keepdims=True), (4, C))
    send_small()

    for copy in hd:
        copy.wait_recv()
    unpack_halo(dp, hd_row, hd_col, hd_cor)

    def image_gradient(wb, _):
        first = pl.multiple_of(wb * 8, 8)
        acc = tap_sums(dp, first, range(RH + 6), taps_all, [jnp.zeros((8, C), F32)] * RH, kb, True)
        for h in range(RH):
            cv[h, pl.ds(first, 8), :] = acc[h]
        return 0

    def finish(wb, _):
        first = pl.multiple_of(wb * 16, 16)
        columns = pl.ds(first, 16)
        for h in range(RH):
            dimg[h, columns, :] = (cot[h, columns, :].astype(F32) + cv[h, columns, :]).astype(BF16)
        return 0

    lax.fori_loop(0, 6, image_gradient, 0)
    send_sums()
    lax.fori_loop(6, 12, image_gradient, 0)
    send_small_sums()
    lax.fori_loop(12, 16, image_gradient, 0)
    lax.fori_loop(0, 8, finish, 0)
    save_part(dimg, d_image_out)
    send_result()
    send_small_result()

    arrived(r1, 3)
    for j in range(NC):
        save_part(a4.at[0, j], g_in_out.at[pl.ds(j * 8, 8)])

    def place(j, _):
        for q in range(4):
            at = pl.multiple_of(j * 32 + q * 8, 8)
            g_out[pl.ds(at, 8), :] = a4[1, j, :, q * 128 : (q + 1) * 128]
        return 0

    lax.fori_loop(0, NC, place, 0)
    save_part(g_out, g_out_out)
    arrived(sa.at[pl.ds(0, XY - 1)], 6)
    for a in range(7):
        g_k[a, pl.ds(0, 4), :] = sa[2 * a]
        g_k[a, pl.ds(4, 3), :] = sa[2 * a + 1][0:3]
    for q in range(4):
        g_b[:, q * 128 : (q + 1) * 128] = sa[14, pl.ds(q, 1), :]
    g_gain[...] = sa[15, pl.ds(0, 1), :]
    save_part(g_k, g_k_out)
    save_part(g_b, g_b_out)
    save_part(g_gain, g_gain_out)

    for copy in hx:
        copy.wait_send()
    for copy in hd:
        copy.wait_send()
    send_in.wait_send()
    send_out.wait_send()
    left_here(from_core, 0)
    left_here(r1, 1)
    left_here(r2.at[pl.ds(0, NR // 2 - 1)], 2)
    left_here(r1, 3)
    left_here(r1s, 4)
    left_here(r2s.at[pl.ds(0, NR - 1)], 5)
    left_here(sa.at[pl.ds(0, XY - 1)], 6)
    for copy in saves:
        copy.wait()


def save(*refs):
    sources, targets, held = refs[:7], refs[7:14], refs[14:21]
    load_sem, save_sem = refs[21:]
    parts = []
    for src, dst, mid in zip(sources, targets, held):
        if src.shape[0] == RH:
            for at in range(0, RH, 4):
                rows = pl.ds(at, 4)
                parts.append((src.at[rows], dst.at[rows], mid.at[rows]))
        else:
            parts.append((src, dst, mid))
    loads = [pltpu.make_async_copy(src, mid, load_sem.at[i]) for i, (src, _, mid) in enumerate(parts)]
    saves = [pltpu.make_async_copy(mid, dst, save_sem.at[i]) for i, (_, dst, mid) in enumerate(parts)]
    for copy in loads:
        copy.start()
    for load, copy in zip(loads, saves):
        load.wait()
        copy.start()
    for copy in saves:
        copy.wait()


def on_device(
    image, dw_kernel, dw_bias, layer_norm_gain, layer_norm_bias, w_in, b_in, w_out, b_out, cotangent
):
    hbm = pl.BlockSpec(memory_space=pltpu.HBM)
    sem = pltpu.SemaphoreType.DMA
    scratch = [
        pltpu.VMEM((RH, CW, C), BF16),
        pltpu.VMEM((RH, CW, C), BF16),
        pltpu.VMEM((HID // 2, C), F32),
        pltpu.VMEM((1, HID), F32),
        pltpu.VMEM((7, 7, C), F32),
        pltpu.VMEM((1, C), F32),
        pltpu.VMEM((RH, CW, C), BF16),
        pltpu.VMEM((RH, CW, C), BF16),
        pltpu.VMEM((7, 7, C), F32),
        pltpu.VMEM((1, C), F32),
        pltpu.VMEM((1, C), F32),
        pltpu.VMEM((1, C), F32),
        pltpu.VMEM((1, HID), F32),
        pltpu.VMEM((1, C), F32),
        pltpu.VMEM((RH + 6, CW + 16, C), F32),
        pltpu.VMEM((RH + 6, CW + 16, C), F32),
        pltpu.VMEM((RH, CW, C), F32),
        pltpu.VMEM((56, 8, C), F32),
        pltpu.VMEM((C, HID), BF16),
        pltpu.VMEM((HID, C), BF16),
        pltpu.VMEM((RH, CW, C), BF16),
        pltpu.VMEM((8, HID), F32),
        pltpu.VMEM((8, C), F32),
        pltpu.VMEM((448, C), F32),
    ]
    for _ in range(2):
        scratch += [
            pltpu.VMEM((2, 3, CW, C), BF16),
            pltpu.VMEM((2, RH, 16, C), BF16),
            pltpu.VMEM((4, 3, 16, C), BF16),
        ]
    scratch += [
        pltpu.VMEM((2, C, HID), F32),
        pltpu.VMEM((C, HID), F32),
        pltpu.VMEM((C, HID), F32),
        pltpu.VMEM((XY - 1, 8, HID), F32),
        pltpu.VMEM((NR // 2, 8, HID), F32),
        pltpu.VMEM((2, NC, 8, HID), F32),
        pltpu.VMEM((XY, 4, C), F32),
        pltpu.VMEM((XY - 1, 4, C), F32),
        pltpu.VMEM((NR, 4, C), F32),
        pltpu.VMEM((XY, 4, C), F32),
        sem((10,)), sem((2,)), sem((2,)), sem((8,)), sem((8,)), sem((8,)), sem((8,)), sem((7,)), sem((7,)), sem((14,)),
    ]
    shapes = (
        jax.ShapeDtypeStruct((RH, CW, C), BF16),
        jax.ShapeDtypeStruct((RH, CW, C), BF16),
        jax.ShapeDtypeStruct((C // 2, HID), F32),
        jax.ShapeDtypeStruct((HID // 2, C), F32),
        jax.ShapeDtypeStruct((1, HID), F32),
        jax.ShapeDtypeStruct((7, 7, C), F32),
        jax.ShapeDtypeStruct((1, C), F32),
    )
    outs = pl.pallas_call(
        kernel,
        out_shape=shapes,
        in_specs=[hbm] * 10,
        out_specs=(hbm,) * 7,
        scratch_shapes=scratch,
        compiler_params=pltpu.CompilerParams(
            collective_id=0, has_side_effects=True, vmem_limit_bytes=63 * 1024 * 1024
        ),
        name="convnext_block",
    )(
        image[0], dw_kernel, dw_bias.reshape(1, C), layer_norm_gain.reshape(1, C), layer_norm_bias.reshape(1, C),
        w_in, b_in.reshape(1, HID), w_out, b_out.reshape(1, C), cotangent[0],
    )
    outs = pl.pallas_call(
        save,
        out_shape=shapes,
        in_specs=[pl.BlockSpec(memory_space=pl.ANY)] * 7,
        out_specs=(hbm,) * 7,
        scratch_shapes=[pltpu.VMEM(x.shape, x.dtype) for x in shapes] + [sem((13,)), sem((13,))],
        compiler_params=pltpu.CompilerParams(vmem_limit_bytes=63 * 1024 * 1024),
        name="save_outputs",
    )(*outs)
    mixed, d_image, g_in, g_out, g_b, g_k, g_gain = outs
    return (mixed[None], d_image[None], g_in, g_out, g_b.reshape(HID), g_k, g_gain.reshape(C))


def solution(mesh):
    return jax.shard_map(
        on_device,
        mesh=mesh,
        in_specs=(
            P("fsdp", "rows", "cols", None),
            P(),
            P(),
            P(),
            P(),
            P("fsdp", None),
            P(),
            P("fsdp", None),
            P(),
            P("fsdp", "rows", "cols", None),
        ),
        out_specs=(
            P("fsdp", "rows", "cols", None),
            P("fsdp", "rows", "cols", None),
            P("fsdp", None),
            P("fsdp", None),
            P(),
            P(),
            P(),
        ),
        check_vma=False,
    )
```

```python
import functools
import math

import jax
import jax.numpy as jnp
from jax import lax
from jax.experimental import pallas as pl
from jax.experimental.pallas import tpu as pltpu
from jax.sharding import PartitionSpec as P

MESH = pl.DeviceIdType.MESH
F32 = jnp.float32
BF16 = jnp.bfloat16

norm_eps = 1e-06
gelu_coef = math.sqrt(2.0 / math.pi)
cubic_coef = 0.044715

RH = 16
CW = 128
C = 128
HID = 512
XY = 16
NR = 16
NC = 8
PIX = RH * CW

NT = (((1,), (1,)), ((), ()))
TN = (((0,), (0,)), ((), ()))


def tap_sums(source, first, rows, taps, acc, kb, flip):
    for b in range(7):
        weights = [kb[(6 - a) * 8 + (6 - b) if flip else a * 8 + b] for a in range(7)]
        for row in rows:
            value = source[row, pl.ds(first + 5 + b, 8), :]
            for h, a in taps(row):
                acc[h] = acc[h] + value * weights[a]
    return acc


def taps_all(row):
    return [(row - a, a) for a in range(7) if 0 <= row - a < RH]


def kernel(
    image, dw_kernel_in, dw_bias_in, gain_in, bias_in, w_in, b_in_in, w_out, b_out_in, cotangent,
    mixed, dimg, g_in, g_out, g_b, g_k, g_gain,
    img, cot, dw_kernel, dw_bias, gain, bias, b_in, b_out, xp, dp, cv, kb, win, wout, dcb,
    bacc, gacc, kacc,
    wide, hx_side, hd_side, hx_row, hx_col, hx_cor, hd_row, hd_col, hd_cor,
    grads, from_core, pair, r1, r2, a4, small, r1s, r2s, sa,
    local_sem, w_send, w_recv, hx_send, hx_recv, hd_send, hd_recv, x_send, x_recv,
):
    mf = lax.axis_index("fsdp")
    mr = lax.axis_index("rows")
    mc = lax.axis_index("cols")
    me = mf * NC + mc
    core = mr % 2
    other = mr + 1 - 2 * core
    mz = mr // 2

    def xy_id(peer):
        return (peer // NC, mr, peer % NC)

    def row_id(peer):
        return (mf, peer, mc)

    up, down = (mr + NR - 1) % NR, (mr + 1) % NR
    left, right = (mc + NC - 1) % NC, (mc + 1) % NC

    loads = [
        (image, img), (cotangent, cot), (dw_kernel_in, dw_kernel), (dw_bias_in, dw_bias), (gain_in, gain), (bias_in, bias),
        (b_in_in, b_in), (b_out_in, b_out), (w_in, win.at[pl.ds(mf * 64, 64)]), (w_out, wout.at[pl.ds(mf * 256, 256)]),
    ]
    loads = [pltpu.make_async_copy(src, dst, local_sem.at[i]) for i, (src, dst) in enumerate(loads)]
    for i in (2, 3, 0, 1, 4, 5, 6, 7, 8, 9):
        loads[i].start()

    barrier = pltpu.get_barrier_semaphore()

    def greet(device):
        pl.semaphore_signal(barrier, inc=1, device_id=device, device_id_type=MESH)

    def greet_xy(k, _):
        greet(xy_id((me + k) % XY))
        return 0

    def greet_rows(k, _):
        greet(row_id((mr + k) % NR))
        return 0

    def greet_other(k, _):
        greet((mf, other, (mc + k) % NC))
        return 0

    beyond = (mr + NR - 1 + 2 * core) % NR
    greet((mf, beyond, left))
    greet((mf, beyond, right))
    lax.fori_loop(1, NC, greet_other, 0)
    lax.fori_loop(1, XY, greet_xy, 0)
    lax.fori_loop(1, NR, greet_rows, 0)

    loads[2].wait()
    loads[3].wait()
    for a in range(7):
        for b in range(7):
            kb[a * 8 + b] = jnp.broadcast_to(dw_kernel[a, pl.ds(b, 1), :], (8, C))
    conv_bias = jnp.broadcast_to(dw_bias[...], (8, C))

    loads[0].wait()

    def widen(r, _):
        xp[3 + r, pl.ds(8, CW), :] = img[r].astype(F32)
        return 0

    lax.fori_loop(0, RH, widen, 0)

    own_rows = range(3, RH + 3)
    edge_rows = (0, 1, 2, RH + 3, RH + 4, RH + 5)

    def conv_inner(wb, _):
        first = pl.multiple_of(wb * 8, 8)
        acc = tap_sums(xp, first, own_rows, taps_all, [conv_bias] * RH, kb, False)
        for h in range(RH):
            cv[h, pl.ds(first, 8), :] = acc[h]
        return 0

    def pack_sides(padded, wide, packed):
        def row(r, _):
            for j in range(3):
                wide[0, j, pl.ds(r, 1), :] = padded[3 + r, pl.ds(CW + 5 + j, 1), :]
                wide[1, j, pl.ds(r, 1), :] = padded[3 + r, pl.ds(8 + j, 1), :]
            return 0

        lax.fori_loop(0, RH, row, 0)
        packed[...] = wide[...].astype(BF16)

    pack_sides(xp, wide, hx_side)
    lax.fori_loop(1, 4, conv_inner, 0)
    pl.semaphore_wait(barrier, 2 + NC - 1 + XY - 1 + NR - 1)

    def halo(source, sides, rows_buf, col_buf, cor_buf, send, recv):
        plan = [
            (source.at[pl.ds(RH - 3, 3)], rows_buf.at[0], (mf, down, mc)),
            (source.at[pl.ds(0, 3)], rows_buf.at[1], (mf, up, mc)),
            (sides.at[0], col_buf.at[0], (mf, mr, right)),
            (sides.at[1], col_buf.at[1], (mf, mr, left)),
            (source.at[pl.ds(RH - 3, 3), pl.ds(CW - 16, 16)], cor_buf.at[0], (mf, down, right)),
            (source.at[pl.ds(RH - 3, 3), pl.ds(0, 16)], cor_buf.at[1], (mf, down, left)),
            (source.at[pl.ds(0, 3), pl.ds(CW - 16, 16)], cor_buf.at[2], (mf, up, right)),
            (source.at[pl.ds(0, 3), pl.ds(0, 16)], cor_buf.at[3], (mf, up, left)),
        ]
        copies = []
        for i, (src, dst, target) in enumerate(plan):
            copy = pltpu.make_async_remote_copy(
                src_ref=src, dst_ref=dst, send_sem=send.at[i], recv_sem=recv.at[i], device_id=target, device_id_type=MESH
            )
            copy.start()
            copies.append(copy)
        return copies

    has_up = jnp.where(mr > 0, 1.0, 0.0).astype(F32)
    has_down = jnp.where(mr < NR - 1, 1.0, 0.0).astype(F32)
    has_left = jnp.where(mc > 0, 1.0, 0.0).astype(F32)
    has_right = jnp.where(mc < NC - 1, 1.0, 0.0).astype(F32)

    def unpack_halo(padded, wide, rows_buf, col_buf, cor_buf):
        for i in range(3):
            padded[i, pl.ds(8, CW), :] = rows_buf[0, i].astype(F32) * has_up
            padded[RH + 3 + i, pl.ds(8, CW), :] = rows_buf[1, i].astype(F32) * has_down
            padded[i, pl.ds(0, 8), :] = cor_buf[0, i].astype(F32)[8:16] * (has_up * has_left)
            padded[i, pl.ds(CW + 8, 8), :] = cor_buf[1, i].astype(F32)[0:8] * (has_up * has_right)
            padded[RH + 3 + i, pl.ds(0, 8), :] = cor_buf[2, i].astype(F32)[8:16] * (has_down * has_left)
            padded[RH + 3 + i, pl.ds(CW + 8, 8), :] = cor_buf[3, i].astype(F32)[0:8] * (has_down * has_right)

        wide[0] = col_buf[0].astype(F32) * has_left
        wide[1] = col_buf[1].astype(F32) * has_right

        def side(r, _):
            for j in range(3):
                padded[3 + r, pl.ds(5 + j, 1), :] = wide[0, j, pl.ds(r, 1), :]
                padded[3 + r, pl.ds(CW + 8 + j, 1), :] = wide[1, j, pl.ds(r, 1), :]
            return 0

        lax.fori_loop(0, RH, side, 0)

    hx = halo(image, hx_side, hx_row, hx_col, hx_cor, hx_send, hx_recv)
    partner = (1 - mf, mr, mc)
    send_in = pltpu.make_async_remote_copy(
        src_ref=w_in, dst_ref=win.at[pl.ds(mf * 64, 64)], send_sem=w_send.at[0], recv_sem=w_recv.at[0],
        device_id=partner, device_id_type=MESH,
    )
    send_in.start()
    send_out = pltpu.make_async_remote_copy(
        src_ref=w_out, dst_ref=wout.at[pl.ds(mf * 256, 256)], send_sem=w_send.at[1], recv_sem=w_recv.at[1],
        device_id=partner, device_id_type=MESH,
    )
    send_out.start()

    lax.fori_loop(4, CW // 8 - 1, conv_inner, 0)

    for copy in hx:
        copy.wait_recv()
    unpack_halo(xp, wide, hx_row, hx_col, hx_cor)

    def conv_edge(wb, _):
        first = pl.multiple_of(wb * 8, 8)
        acc = [None] * RH
        touched = (0, 1, 2, RH - 3, RH - 2, RH - 1)
        for h in touched:
            acc[h] = cv[h, pl.ds(first, 8), :]
        acc = tap_sums(xp, first, edge_rows, taps_all, acc, kb, False)
        for h in touched:
            cv[h, pl.ds(first, 8), :] = acc[h]
        return 0

    lax.fori_loop(1, CW // 8 - 1, conv_edge, 0)

    def conv_side(i, _):
        first = pl.multiple_of(i * (CW - 8), 8)
        acc = tap_sums(xp, first, range(RH + 6), taps_all, [conv_bias] * RH, kb, False)
        for h in range(RH):
            cv[h, pl.ds(first, 8), :] = acc[h]
        return 0

    lax.fori_loop(0, 2, conv_side, 0)

    for i in (1, 4, 5, 6, 7, 8, 9):
        loads[i].wait()
    send_in.wait_recv()
    send_out.wait_recv()
    def remote(src, dst, sem, device):
        return pltpu.make_async_remote_copy(
            src_ref=src, dst_ref=dst, send_sem=x_send.at[sem], recv_sem=x_recv.at[sem], device_id=device, device_id_type=MESH
        )

    def start(copies):
        for copy in copies:
            copy.start()

    def arrived(ref, sem):
        pltpu.make_async_copy(ref, ref, x_recv.at[sem]).wait()

    def left_here(ref, sem):
        pltpu.make_async_copy(ref, ref, x_send.at[sem]).wait()

    far_xy = (10, 6, 2, 14, 8, 9, 11, 7, 12, 4, 5, 13, 3, 1, 15)
    far_z = (4, 3, 5, 2, 6, 1, 7)
    far_rows = (8, 7, 9, 6, 10, 5, 11, 4, 12, 3, 13, 2, 14, 1, 15)
    far_cols = (6, 2, 4, 5, 7, 3, 1)

    conv = cv[...].reshape(PIX, C)
    center = jnp.mean(conv, axis=-1, keepdims=True)
    spread = conv - center
    rstd = lax.rsqrt(jnp.mean(spread * spread, axis=-1, keepdims=True) + norm_eps)
    xhat = spread * rstd
    normed = (xhat * gain[...] + bias[...]).astype(BF16)
    upstream = cot[...].reshape(PIX, C)
    pre = jnp.dot(normed, win[...], preferred_element_type=F32) + b_in[...]
    square = pre * pre
    tanh_val = jnp.tanh(pre * (gelu_coef + (gelu_coef * cubic_coef) * square))
    half_gate = 0.5 + 0.5 * tanh_val
    hidden = (pre * half_gate).astype(BF16)
    slope = half_gate + (pre * (0.5 - 0.5 * tanh_val * tanh_val)) * (
        gelu_coef + (3.0 * gelu_coef * cubic_coef) * square
    )
    d_wide = lax.dot_general(upstream, wout[...], NT, preferred_element_type=F32) * slope
    d_pre = d_wide.astype(BF16)
    bacc[...] = jnp.sum(d_wide.reshape(PIX // 8, 8, HID), axis=0)

    grads[0] = lax.dot_general(normed, d_pre, TN, preferred_element_type=F32)
    out_turned = lax.dot_general(upstream, hidden, TN, preferred_element_type=F32)
    for q in range(4):
        turned = out_turned[:, q * 128 : (q + 1) * 128].T
        for u in range(16):
            p, at = q * 4 + u // 4, u % 4
            grads[1, p * 8 : (p + 1) * 8, at * 128 : (at + 1) * 128] = turned[u * 8 : (u + 1) * 8]
    start([remote(grads.at[1 - core], from_core, 0, (mf, other, mc))])

    dn = lax.dot_general(d_pre, win[...], NT, preferred_element_type=F32)
    gacc[...] = jnp.sum((dn * xhat).reshape(PIX // 8, 8, C), axis=0)
    q = dn * gain[...]
    d_conv = (
        rstd * (q - jnp.mean(q, axis=-1, keepdims=True) - xhat * jnp.mean(q * xhat, axis=-1, keepdims=True))
    ).astype(BF16)
    d_rows = d_conv.reshape(RH, CW, C)
    dcb[...] = d_rows
    dp[pl.ds(3, RH), pl.ds(8, CW), :] = d_rows.astype(F32)

    pack_sides(dp, wide, hd_side)
    hd = halo(dcb, hd_side, hd_row, hd_col, hd_cor, hd_send, hd_recv)

    def send_pair():
        arrived(from_core, 0)

        def add(p, _):
            rows = pl.ds(pl.multiple_of(p * 8, 8), 8)
            pair[rows, :] = grads[core, rows, :] + from_core[rows, :]
            return 0

        lax.fori_loop(0, XY, add, 0)
        copies = []
        for k in far_xy:
            peer = (me + k) % XY
            rows = pl.ds(pl.multiple_of(peer * 8, 8), 8)
            copies.append(remote(pair.at[rows], r1.at[k - 1], 1, xy_id(peer)))
        start(copies)

    def send_sums():
        arrived(r1, 1)
        total = pair[pl.ds(pl.multiple_of(me * 8, 8), 8), :]
        for k in range(XY - 1):
            total = total + r1[k]
        r2[mz] = total
        start([remote(r2.at[mz], r2.at[mz], 2, row_id((mr + 2 * k) % NR)) for k in far_z])

    def send_result():
        arrived(r2.at[pl.ds(0, NR // 2 - 1)], 2)
        total = r2[0]
        for z in range(1, NR // 2):
            total = total + r2[z]
        a4[core, mc] = total
        copies = []
        for k in far_cols:
            for row in (other, mr):
                copies.append(remote(a4.at[core, mc], a4.at[core, mc], 3, (mf, row, (mc + k) % NC)))
        copies.append(remote(a4.at[core, mc], a4.at[core, mc], 3, (mf, other, mc)))
        start(copies)

    def send_small():
        start([remote(small.at[(me + k) % XY], r1s.at[k - 1], 4, xy_id((me + k) % XY)) for k in far_xy])

    def send_small_sums():
        arrived(r1s, 4)
        total = small[me]
        for k in range(XY - 1):
            total = total + r1s[k]
        r2s[mr] = total
        start([remote(r2s.at[mr], r2s.at[mr], 5, row_id((mr + k) % NR)) for k in far_rows])

    def send_small_result():
        arrived(r2s.at[pl.ds(0, NR - 1)], 5)
        total = r2s[0]
        for r in range(1, NR):
            total = total + r2s[r]
        sa[me] = total
        start([remote(sa.at[me], sa.at[me], 6, xy_id((me + k) % XY)) for k in far_xy])

    def tap_gradient(b):
        def step(wb, acc):
            first = pl.multiple_of(wb * 8, 8)
            acc = list(acc)
            grad = [dp[3 + h, pl.ds(first + 8, 8), :] for h in range(RH)]
            for row in range(RH + 6):
                value = xp[row, pl.ds(first + 5 + b, 8), :]
                for h, a in taps_all(row):
                    acc[a] = acc[a] + value * grad[h]
            return tuple(acc)

        acc = lax.fori_loop(0, CW // 8, step, tuple(jnp.zeros((8, C), F32) for _ in range(7)), unroll=4)
        for a in range(7):
            kacc[pl.ds((a * 8 + b) * 8, 8), :] = acc[a]

    for b in range(7):
        if b == 3:
            send_pair()
        tap_gradient(b)
    for a in range(7):
        kacc[pl.ds((a * 8 + 7) * 8, 8), :] = jnp.zeros((8, C), F32)
    for a in range(7):
        total = kacc[pl.ds(a * 64, 8, stride=8), :]
        for s in range(1, 8):
            total = total + kacc[pl.ds(a * 64 + s, 8, stride=8), :]
        small[2 * a] = total[0:4]
        small[2 * a + 1] = total[4:8]
    for q in range(4):
        small[14, pl.ds(q, 1), :] = jnp.sum(bacc[:, q * 128 : (q + 1) * 128], axis=0, keepdims=True)
    small[15] = jnp.broadcast_to(jnp.sum(gacc[...], axis=0, keepdims=True), (4, C))
    send_small()

    out_sum = jnp.dot(hidden, wout[...], preferred_element_type=F32)
    field = img[...].reshape(PIX, C).astype(F32)
    mixed[...] = (field + out_sum + b_out[...]).astype(BF16).reshape(RH, CW, C)

    for copy in hd:
        copy.wait_recv()
    unpack_halo(dp, wide, hd_row, hd_col, hd_cor)

    def image_gradient(wb, _):
        first = pl.multiple_of(wb * 8, 8)
        acc = tap_sums(dp, first, range(RH + 6), taps_all, [jnp.zeros((8, C), F32)] * RH, kb, True)
        for h in range(RH):
            cv[h, pl.ds(first, 8), :] = acc[h]
        return 0

    def finish(wb, _):
        first = pl.multiple_of(wb * 16, 16)
        columns = pl.ds(first, 16)
        for h in range(RH):
            dimg[h, columns, :] = (cot[h, columns, :].astype(F32) + cv[h, columns, :]).astype(BF16)
        return 0

    lax.fori_loop(0, 6, image_gradient, 0)
    send_sums()
    lax.fori_loop(6, 12, image_gradient, 0)
    send_small_sums()
    lax.fori_loop(12, 16, image_gradient, 0)
    lax.fori_loop(0, 8, finish, 0)
    send_result()
    send_small_result()

    arrived(r1, 3)
    def place(j, _):
        for q in range(4):
            at = pl.multiple_of(j * 32 + q * 8, 8)
            g_out[pl.ds(at, 8), :] = a4[1, j, :, q * 128 : (q + 1) * 128]
        g_in[pl.ds(pl.multiple_of(j * 8, 8), 8), :] = a4[0, j]
        return 0

    lax.fori_loop(0, NC, place, 0)
    arrived(sa.at[pl.ds(0, XY - 1)], 6)
    for a in range(7):
        g_k[a, pl.ds(0, 4), :] = sa[2 * a]
        g_k[a, pl.ds(4, 3), :] = sa[2 * a + 1][0:3]
    for q in range(4):
        g_b[:, q * 128 : (q + 1) * 128] = sa[14, pl.ds(q, 1), :]
    g_gain[...] = sa[15, pl.ds(0, 1), :]

    for copy in hx:
        copy.wait_send()
    for copy in hd:
        copy.wait_send()
    send_in.wait_send()
    send_out.wait_send()
    left_here(from_core, 0)
    left_here(r1, 1)
    left_here(r2.at[pl.ds(0, NR // 2 - 1)], 2)
    left_here(r1, 3)
    left_here(r1s, 4)
    left_here(r2s.at[pl.ds(0, NR - 1)], 5)
    left_here(sa.at[pl.ds(0, XY - 1)], 6)


def save(*refs):
    sources, targets, sem = refs[:7], refs[7:14], refs[14]
    copies = [pltpu.make_async_copy(src, dst, sem.at[i]) for i, (src, dst) in enumerate(zip(sources, targets))]
    for copy in copies:
        copy.start()
    for copy in copies:
        copy.wait()


def on_device(
    image, dw_kernel, dw_bias, layer_norm_gain, layer_norm_bias, w_in, b_in, w_out, b_out, cotangent
):
    hbm = pl.BlockSpec(memory_space=pltpu.HBM)
    sem = pltpu.SemaphoreType.DMA
    scratch = [
        pltpu.VMEM((RH, CW, C), BF16),
        pltpu.VMEM((RH, CW, C), BF16),
        pltpu.VMEM((7, 7, C), F32),
        pltpu.VMEM((1, C), F32),
        pltpu.VMEM((1, C), F32),
        pltpu.VMEM((1, C), F32),
        pltpu.VMEM((1, HID), F32),
        pltpu.VMEM((1, C), F32),
        pltpu.VMEM((RH + 6, CW + 16, C), F32),
        pltpu.VMEM((RH + 6, CW + 16, C), F32),
        pltpu.VMEM((RH, CW, C), F32),
        pltpu.VMEM((56, 8, C), F32),
        pltpu.VMEM((C, HID), BF16),
        pltpu.VMEM((HID, C), BF16),
        pltpu.VMEM((RH, CW, C), BF16),
        pltpu.VMEM((8, HID), F32),
        pltpu.VMEM((8, C), F32),
        pltpu.VMEM((448, C), F32),
    ]
    scratch += [
        pltpu.VMEM((2, 3, RH, C), F32),
        pltpu.VMEM((2, 3, RH, C), BF16),
        pltpu.VMEM((2, 3, RH, C), BF16),
    ]
    for _ in range(2):
        scratch += [
            pltpu.VMEM((2, 3, CW, C), BF16),
            pltpu.VMEM((2, 3, RH, C), BF16),
            pltpu.VMEM((4, 3, 16, C), BF16),
        ]
    scratch += [
        pltpu.VMEM((2, C, HID), F32),
        pltpu.VMEM((C, HID), F32),
        pltpu.VMEM((C, HID), F32),
        pltpu.VMEM((XY - 1, 8, HID), F32),
        pltpu.VMEM((NR // 2, 8, HID), F32),
        pltpu.VMEM((2, NC, 8, HID), F32),
        pltpu.VMEM((XY, 4, C), F32),
        pltpu.VMEM((XY - 1, 4, C), F32),
        pltpu.VMEM((NR, 4, C), F32),
        pltpu.VMEM((XY, 4, C), F32),
        sem((10,)), sem((2,)), sem((2,)), sem((8,)), sem((8,)), sem((8,)), sem((8,)), sem((7,)), sem((7,)),
    ]
    shapes = (
        jax.ShapeDtypeStruct((RH, CW, C), BF16),
        jax.ShapeDtypeStruct((RH, CW, C), BF16),
        jax.ShapeDtypeStruct((C // 2, HID), F32),
        jax.ShapeDtypeStruct((HID // 2, C), F32),
        jax.ShapeDtypeStruct((1, HID), F32),
        jax.ShapeDtypeStruct((7, 7, C), F32),
        jax.ShapeDtypeStruct((1, C), F32),
    )
    operands = (
        image[0], dw_kernel, dw_bias.reshape(1, C), layer_norm_gain.reshape(1, C), layer_norm_bias.reshape(1, C),
        w_in, b_in.reshape(1, HID), w_out, b_out.reshape(1, C), cotangent[0],
    )
    outs = pl.pallas_call(
        kernel,
        out_shape=tuple(pltpu.VMEM(x.shape, x.dtype) for x in shapes),
        in_specs=[hbm] * 10,
        out_specs=(pl.BlockSpec(memory_space=pltpu.VMEM),) * 7,
        scratch_shapes=scratch,
        compiler_params=pltpu.CompilerParams(
            collective_id=0, has_side_effects=True, vmem_limit_bytes=48 * 1024 * 1024
        ),
        name="convnext_block",
    )(*[pltpu.with_memory_space_constraint(x, pltpu.HBM) for x in operands])
    outs = pl.pallas_call(
        save,
        out_shape=shapes,
        in_specs=[pl.BlockSpec(memory_space=pl.ANY)] * 7,
        out_specs=(hbm,) * 7,
        scratch_shapes=[sem((7,))],
        name="save_outputs",
    )(*[pltpu.with_memory_space_constraint(x, pltpu.VMEM) for x in outs])
    mixed, d_image, g_in, g_out, g_b, g_k, g_gain = outs
    return (mixed[None], d_image[None], g_in, g_out, g_b.reshape(HID), g_k, g_gain.reshape(C))


def solution(mesh):
    return jax.shard_map(
        on_device,
        mesh=mesh,
        in_specs=(
            P("fsdp", "rows", "cols", None),
            P(),
            P(),
            P(),
            P(),
            P("fsdp", None),
            P(),
            P("fsdp", None),
            P(),
            P("fsdp", "rows", "cols", None),
        ),
        out_specs=(
            P("fsdp", "rows", "cols", None),
            P("fsdp", "rows", "cols", None),
            P("fsdp", None),
            P("fsdp", None),
            P(),
            P(),
            P(),
        ),
        check_vma=False,
    )
```

```python
import functools
import math

import jax
import jax.numpy as jnp
from jax import lax
from jax.experimental import pallas as pl
from jax.experimental.pallas import tpu as pltpu
from jax.sharding import PartitionSpec as P

MESH = pl.DeviceIdType.MESH
F32 = jnp.float32
BF16 = jnp.bfloat16

norm_eps = 1e-06
gelu_coef = math.sqrt(2.0 / math.pi)
cubic_coef = 0.044715

RH = 16
CW = 128
C = 128
HID = 512
XY = 16
NR = 16
NC = 8
PIX = RH * CW

NT = (((1,), (1,)), ((), ()))
TN = (((0,), (0,)), ((), ()))


def tap_sums(source, first, rows, taps, acc, kb, flip):
    for b in range(7):
        weights = [kb[(6 - a) * 8 + (6 - b) if flip else a * 8 + b] for a in range(7)]
        for row in rows:
            value = source[row, pl.ds(first + 5 + b, 8), :]
            for h, a in taps(row):
                acc[h] = acc[h] + value * weights[a]
    return acc


def taps_all(row):
    return [(row - a, a) for a in range(7) if 0 <= row - a < RH]


def kernel(
    image, dw_kernel_in, dw_bias_in, gain_in, bias_in, w_in, b_in_in, w_out, b_out_in, cotangent,
    mixed, dimg, g_in, g_out, g_b, g_k, g_gain,
    img, cot, dw_kernel, dw_bias, gain, bias, b_in, b_out, xp, dp, cv, kb, win, wout, dcb,
    bacc, gacc, kacc,
    wide, hx_side, hd_side, hx_row, hx_col, hx_cor, hd_row, hd_col, hd_cor,
    grads, from_core, pair, r1, r2, a4, small, r1s, r2s, sa,
    local_sem, w_send, w_recv, hx_send, hx_recv, hd_send, hd_recv, x_send, x_recv,
):
    mf = lax.axis_index("fsdp")
    mr = lax.axis_index("rows")
    mc = lax.axis_index("cols")
    me = mf * NC + mc
    core = mr % 2
    other = mr + 1 - 2 * core
    mz = mr // 2

    def xy_id(peer):
        return (peer // NC, mr, peer % NC)

    def row_id(peer):
        return (mf, peer, mc)

    up, down = (mr + NR - 1) % NR, (mr + 1) % NR
    left, right = (mc + NC - 1) % NC, (mc + 1) % NC

    loads = [
        (image, img), (cotangent, cot), (dw_kernel_in, dw_kernel), (dw_bias_in, dw_bias), (gain_in, gain), (bias_in, bias),
        (b_in_in, b_in), (b_out_in, b_out), (w_in, win.at[pl.ds(mf * 64, 64)]), (w_out, wout.at[pl.ds(mf * 256, 256)]),
    ]
    loads = [pltpu.make_async_copy(src, dst, local_sem.at[i]) for i, (src, dst) in enumerate(loads)]
    for i in (2, 3, 0, 1, 4, 5, 6, 7, 8, 9):
        loads[i].start()

    barrier = pltpu.get_barrier_semaphore()

    def greet(device):
        pl.semaphore_signal(barrier, inc=1, device_id=device, device_id_type=MESH)

    def greet_xy(k, _):
        greet(xy_id((me + k) % XY))
        return 0

    def greet_rows(k, _):
        greet(row_id((mr + k) % NR))
        return 0

    def greet_other(k, _):
        greet((mf, other, (mc + k) % NC))
        return 0

    beyond = (mr + NR - 1 + 2 * core) % NR
    greet((mf, beyond, left))
    greet((mf, beyond, right))
    lax.fori_loop(1, NC, greet_other, 0)
    lax.fori_loop(1, XY, greet_xy, 0)
    lax.fori_loop(1, NR, greet_rows, 0)

    loads[2].wait()
    loads[3].wait()
    for a in range(7):
        for b in range(7):
            kb[a * 8 + b] = jnp.broadcast_to(dw_kernel[a, pl.ds(b, 1), :], (8, C))
    conv_bias = jnp.broadcast_to(dw_bias[...], (8, C))

    loads[0].wait()

    def widen(r, _):
        xp[3 + r, pl.ds(8, CW), :] = img[r].astype(F32)
        return 0

    lax.fori_loop(0, RH, widen, 0)

    own_rows = range(3, RH + 3)
    edge_rows = (0, 1, 2, RH + 3, RH + 4, RH + 5)

    def conv_inner(wb, _):
        first = pl.multiple_of(wb * 8, 8)
        acc = tap_sums(xp, first, own_rows, taps_all, [conv_bias] * RH, kb, False)
        for h in range(RH):
            cv[h, pl.ds(first, 8), :] = acc[h]
        return 0

    def pack_sides(padded, wide, packed):
        def row(r, _):
            for j in range(3):
                wide[0, j, pl.ds(r, 1), :] = padded[3 + r, pl.ds(CW + 5 + j, 1), :]
                wide[1, j, pl.ds(r, 1), :] = padded[3 + r, pl.ds(8 + j, 1), :]
            return 0

        lax.fori_loop(0, RH, row, 0)
        packed[...] = wide[...].astype(BF16)

    pack_sides(xp, wide, hx_side)
    lax.fori_loop(1, 4, conv_inner, 0)
    pl.semaphore_wait(barrier, 2 + NC - 1 + XY - 1 + NR - 1)

    def halo(source, sides, rows_buf, col_buf, cor_buf, send, recv):
        plan = [
            (source.at[pl.ds(RH - 3, 3)], rows_buf.at[0], (mf, down, mc)),
            (source.at[pl.ds(0, 3)], rows_buf.at[1], (mf, up, mc)),
            (sides.at[0], col_buf.at[0], (mf, mr, right)),
            (sides.at[1], col_buf.at[1], (mf, mr, left)),
            (source.at[pl.ds(RH - 3, 3), pl.ds(CW - 16, 16)], cor_buf.at[0], (mf, down, right)),
            (source.at[pl.ds(RH - 3, 3), pl.ds(0, 16)], cor_buf.at[1], (mf, down, left)),
            (source.at[pl.ds(0, 3), pl.ds(CW - 16, 16)], cor_buf.at[2], (mf, up, right)),
            (source.at[pl.ds(0, 3), pl.ds(0, 16)], cor_buf.at[3], (mf, up, left)),
        ]
        copies = []
        for i, (src, dst, target) in enumerate(plan):
            copy = pltpu.make_async_remote_copy(
                src_ref=src, dst_ref=dst, send_sem=send.at[i], recv_sem=recv.at[i], device_id=target, device_id_type=MESH
            )
            copy.start()
            copies.append(copy)
        return copies

    has_up = jnp.where(mr > 0, 1.0, 0.0).astype(F32)
    has_down = jnp.where(mr < NR - 1, 1.0, 0.0).astype(F32)
    has_left = jnp.where(mc > 0, 1.0, 0.0).astype(F32)
    has_right = jnp.where(mc < NC - 1, 1.0, 0.0).astype(F32)

    def unpack_halo(padded, wide, rows_buf, col_buf, cor_buf):
        for i in range(3):
            padded[i, pl.ds(8, CW), :] = rows_buf[0, i].astype(F32) * has_up
            padded[RH + 3 + i, pl.ds(8, CW), :] = rows_buf[1, i].astype(F32) * has_down
            padded[i, pl.ds(0, 8), :] = cor_buf[0, i].astype(F32)[8:16] * (has_up * has_left)
            padded[i, pl.ds(CW + 8, 8), :] = cor_buf[1, i].astype(F32)[0:8] * (has_up * has_right)
            padded[RH + 3 + i, pl.ds(0, 8), :] = cor_buf[2, i].astype(F32)[8:16] * (has_down * has_left)
            padded[RH + 3 + i, pl.ds(CW + 8, 8), :] = cor_buf[3, i].astype(F32)[0:8] * (has_down * has_right)

        wide[0] = col_buf[0].astype(F32) * has_left
        wide[1] = col_buf[1].astype(F32) * has_right

        def side(r, _):
            for j in range(3):
                padded[3 + r, pl.ds(5 + j, 1), :] = wide[0, j, pl.ds(r, 1), :]
                padded[3 + r, pl.ds(CW + 8 + j, 1), :] = wide[1, j, pl.ds(r, 1), :]
            return 0

        lax.fori_loop(0, RH, side, 0)

    hx = halo(image, hx_side, hx_row, hx_col, hx_cor, hx_send, hx_recv)
    partner = (1 - mf, mr, mc)
    send_in = pltpu.make_async_remote_copy(
        src_ref=w_in, dst_ref=win.at[pl.ds(mf * 64, 64)], send_sem=w_send.at[0], recv_sem=w_recv.at[0],
        device_id=partner, device_id_type=MESH,
    )
    send_in.start()
    send_out = pltpu.make_async_remote_copy(
        src_ref=w_out, dst_ref=wout.at[pl.ds(mf * 256, 256)], send_sem=w_send.at[1], recv_sem=w_recv.at[1],
        device_id=partner, device_id_type=MESH,
    )
    send_out.start()

    lax.fori_loop(4, CW // 8 - 1, conv_inner, 0)

    for copy in hx:
        copy.wait_recv()
    unpack_halo(xp, wide, hx_row, hx_col, hx_cor)

    def conv_edge(wb, _):
        first = pl.multiple_of(wb * 8, 8)
        acc = [None] * RH
        touched = (0, 1, 2, RH - 3, RH - 2, RH - 1)
        for h in touched:
            acc[h] = cv[h, pl.ds(first, 8), :]
        acc = tap_sums(xp, first, edge_rows, taps_all, acc, kb, False)
        for h in touched:
            cv[h, pl.ds(first, 8), :] = acc[h]
        return 0

    lax.fori_loop(1, CW // 8 - 1, conv_edge, 0)

    def conv_side(i, _):
        first = pl.multiple_of(i * (CW - 8), 8)
        acc = tap_sums(xp, first, range(RH + 6), taps_all, [conv_bias] * RH, kb, False)
        for h in range(RH):
            cv[h, pl.ds(first, 8), :] = acc[h]
        return 0

    lax.fori_loop(0, 2, conv_side, 0)

    for i in (1, 4, 5, 6, 7, 8, 9):
        loads[i].wait()
    send_in.wait_recv()
    send_out.wait_recv()
    def remote(src, dst, sem, device):
        return pltpu.make_async_remote_copy(
            src_ref=src, dst_ref=dst, send_sem=x_send.at[sem], recv_sem=x_recv.at[sem], device_id=device, device_id_type=MESH
        )

    def start(copies):
        for copy in copies:
            copy.start()

    def arrived(ref, sem):
        pltpu.make_async_copy(ref, ref, x_recv.at[sem]).wait()

    def left_here(ref, sem):
        pltpu.make_async_copy(ref, ref, x_send.at[sem]).wait()

    far_xy = (10, 6, 2, 14, 8, 9, 11, 7, 12, 4, 5, 13, 3, 1, 15)
    far_z = (4, 3, 5, 2, 6, 1, 7)
    far_rows = (8, 7, 9, 6, 10, 5, 11, 4, 12, 3, 13, 2, 14, 1, 15)
    far_cols = (6, 2, 4, 5, 7, 3, 1)

    conv = cv[...].reshape(PIX, C)
    center = jnp.mean(conv, axis=-1, keepdims=True)
    spread = conv - center
    rstd = lax.rsqrt(jnp.mean(spread * spread, axis=-1, keepdims=True) + norm_eps)
    xhat = spread * rstd
    normed = (xhat * gain[...] + bias[...]).astype(BF16)
    upstream = cot[...].reshape(PIX, C)
    pre = jnp.dot(normed, win[...], preferred_element_type=F32) + b_in[...]
    square = pre * pre
    tanh_val = jnp.tanh(pre * (gelu_coef + (gelu_coef * cubic_coef) * square))
    half_gate = 0.5 + 0.5 * tanh_val
    hidden = (pre * half_gate).astype(BF16)
    slope = half_gate + (pre * (0.5 - 0.5 * tanh_val * tanh_val)) * (
        gelu_coef + (3.0 * gelu_coef * cubic_coef) * square
    )
    d_wide = lax.dot_general(upstream, wout[...], NT, preferred_element_type=F32) * slope
    d_pre = d_wide.astype(BF16)
    bacc[...] = jnp.sum(d_wide.reshape(PIX // 8, 8, HID), axis=0)

    grads[0] = lax.dot_general(normed, d_pre, TN, preferred_element_type=F32)
    out_turned = lax.dot_general(upstream, hidden, TN, preferred_element_type=F32)
    for q in range(4):
        turned = out_turned[:, q * 128 : (q + 1) * 128].T
        for u in range(16):
            p, at = q * 4 + u // 4, u % 4
            grads[1, p * 8 : (p + 1) * 8, at * 128 : (at + 1) * 128] = turned[u * 8 : (u + 1) * 8]

    dn = lax.dot_general(d_pre, win[...], NT, preferred_element_type=F32)
    gacc[...] = jnp.sum((dn * xhat).reshape(PIX // 8, 8, C), axis=0)
    q = dn * gain[...]
    d_conv = (
        rstd * (q - jnp.mean(q, axis=-1, keepdims=True) - xhat * jnp.mean(q * xhat, axis=-1, keepdims=True))
    ).astype(BF16)
    d_rows = d_conv.reshape(RH, CW, C)
    dcb[...] = d_rows
    dp[pl.ds(3, RH), pl.ds(8, CW), :] = d_rows.astype(F32)

    start([remote(grads.at[1 - core], from_core, 0, (mf, other, mc))])
    pack_sides(dp, wide, hd_side)
    hd = halo(dcb, hd_side, hd_row, hd_col, hd_cor, hd_send, hd_recv)

    def send_pair():
        arrived(from_core, 0)

        def add(p, _):
            rows = pl.ds(pl.multiple_of(p * 8, 8), 8)
            pair[rows, :] = grads[core, rows, :] + from_core[rows, :]
            return 0

        lax.fori_loop(0, XY, add, 0)
        copies = []
        for k in far_xy:
            peer = (me + k) % XY
            rows = pl.ds(pl.multiple_of(peer * 8, 8), 8)
            copies.append(remote(pair.at[rows], r1.at[k - 1], 1, xy_id(peer)))
        start(copies)

    def send_sums():
        arrived(r1, 1)
        total = pair[pl.ds(pl.multiple_of(me * 8, 8), 8), :]
        for k in range(XY - 1):
            total = total + r1[k]
        r2[mz] = total
        start([remote(r2.at[mz], r2.at[mz], 2, row_id((mr + 2 * k) % NR)) for k in far_z])

    def send_result():
        arrived(r2.at[pl.ds(0, NR // 2 - 1)], 2)
        total = r2[0]
        for z in range(1, NR // 2):
            total = total + r2[z]
        a4[core, mc] = total
        copies = []
        for k in far_cols:
            for row in (other, mr):
                copies.append(remote(a4.at[core, mc], a4.at[core, mc], 3, (mf, row, (mc + k) % NC)))
        copies.append(remote(a4.at[core, mc], a4.at[core, mc], 3, (mf, other, mc)))
        start(copies)

    def send_small():
        start([remote(small.at[(me + k) % XY], r1s.at[k - 1], 4, xy_id((me + k) % XY)) for k in far_xy])

    def send_small_sums():
        arrived(r1s, 4)
        total = small[me]
        for k in range(XY - 1):
            total = total + r1s[k]
        r2s[mr] = total
        start([remote(r2s.at[mr], r2s.at[mr], 5, row_id((mr + k) % NR)) for k in far_rows])

    def send_small_result():
        arrived(r2s.at[pl.ds(0, NR - 1)], 5)
        total = r2s[0]
        for r in range(1, NR):
            total = total + r2s[r]
        sa[me] = total
        start([remote(sa.at[me], sa.at[me], 6, xy_id((me + k) % XY)) for k in far_xy])

    def tap_gradient(taps, unroll):
        def step(wb, acc):
            first = pl.multiple_of(wb * 8, 8)
            acc = list(acc)
            grad = [dp[3 + h, pl.ds(first + 8, 8), :] for h in range(RH)]
            for i, b in enumerate(taps):
                for row in range(RH + 6):
                    value = xp[row, pl.ds(first + 5 + b, 8), :]
                    for h, a in taps_all(row):
                        acc[i * 7 + a] = acc[i * 7 + a] + value * grad[h]
            return tuple(acc)

        zero = jnp.zeros((8, C), F32)
        acc = lax.fori_loop(0, CW // 8, step, (zero,) * (7 * len(taps)), unroll=unroll)
        for i, b in enumerate(taps):
            for a in range(7):
                kacc[pl.ds((a * 8 + b) * 8, 8), :] = acc[i * 7 + a]

    tap_gradient((0, 1), 2)
    send_pair()
    tap_gradient((2, 3), 2)
    tap_gradient((4, 5), 2)
    tap_gradient((6,), 4)
    for a in range(7):
        kacc[pl.ds((a * 8 + 7) * 8, 8), :] = jnp.zeros((8, C), F32)
    for a in range(7):
        total = kacc[pl.ds(a * 64, 8, stride=8), :]
        for s in range(1, 8):
            total = total + kacc[pl.ds(a * 64 + s, 8, stride=8), :]
        small[2 * a] = total[0:4]
        small[2 * a + 1] = total[4:8]
    for q in range(4):
        small[14, pl.ds(q, 1), :] = jnp.sum(bacc[:, q * 128 : (q + 1) * 128], axis=0, keepdims=True)
    small[15] = jnp.broadcast_to(jnp.sum(gacc[...], axis=0, keepdims=True), (4, C))
    send_small()


    for copy in hd:
        copy.wait_recv()
    unpack_halo(dp, wide, hd_row, hd_col, hd_cor)

    def image_gradient(wb, _):
        first = pl.multiple_of(wb * 8, 8)
        acc = tap_sums(dp, first, range(RH + 6), taps_all, [jnp.zeros((8, C), F32)] * RH, kb, True)
        for h in range(RH):
            cv[h, pl.ds(first, 8), :] = acc[h]
        return 0

    def finish(wb, _):
        first = pl.multiple_of(wb * 16, 16)
        columns = pl.ds(first, 16)
        for h in range(RH):
            dimg[h, columns, :] = (cot[h, columns, :].astype(F32) + cv[h, columns, :]).astype(BF16)
        return 0

    lax.fori_loop(0, 4, image_gradient, 0)
    send_sums()
    lax.fori_loop(4, 8, image_gradient, 0)
    send_small_sums()
    lax.fori_loop(8, 16, image_gradient, 0)
    out_sum = jnp.dot(hidden, wout[...], preferred_element_type=F32)
    field = img[...].reshape(PIX, C).astype(F32)
    mixed[...] = (field + out_sum + b_out[...]).astype(BF16).reshape(RH, CW, C)
    lax.fori_loop(0, 8, finish, 0)
    send_result()
    send_small_result()

    arrived(r1, 3)
    def place(j, _):
        for q in range(4):
            at = pl.multiple_of(j * 32 + q * 8, 8)
            g_out[pl.ds(at, 8), :] = a4[1, j, :, q * 128 : (q + 1) * 128]
        g_in[pl.ds(pl.multiple_of(j * 8, 8), 8), :] = a4[0, j]
        return 0

    lax.fori_loop(0, NC, place, 0)
    arrived(sa.at[pl.ds(0, XY - 1)], 6)
    for a in range(7):
        g_k[a, pl.ds(0, 4), :] = sa[2 * a]
        g_k[a, pl.ds(4, 3), :] = sa[2 * a + 1][0:3]
    for q in range(4):
        g_b[:, q * 128 : (q + 1) * 128] = sa[14, pl.ds(q, 1), :]
    g_gain[...] = sa[15, pl.ds(0, 1), :]

    for copy in hx:
        copy.wait_send()
    for copy in hd:
        copy.wait_send()
    send_in.wait_send()
    send_out.wait_send()
    left_here(from_core, 0)
    left_here(r1, 1)
    left_here(r2.at[pl.ds(0, NR // 2 - 1)], 2)
    left_here(r1, 3)
    left_here(r1s, 4)
    left_here(r2s.at[pl.ds(0, NR - 1)], 5)
    left_here(sa.at[pl.ds(0, XY - 1)], 6)


def save(*refs):
    sources, targets, sem = refs[:7], refs[7:14], refs[14]
    copies = [pltpu.make_async_copy(src, dst, sem.at[i]) for i, (src, dst) in enumerate(zip(sources, targets))]
    for copy in copies:
        copy.start()
    for copy in copies:
        copy.wait()


def on_device(
    image, dw_kernel, dw_bias, layer_norm_gain, layer_norm_bias, w_in, b_in, w_out, b_out, cotangent
):
    hbm = pl.BlockSpec(memory_space=pltpu.HBM)
    sem = pltpu.SemaphoreType.DMA
    scratch = [
        pltpu.VMEM((RH, CW, C), BF16),
        pltpu.VMEM((RH, CW, C), BF16),
        pltpu.VMEM((7, 7, C), F32),
        pltpu.VMEM((1, C), F32),
        pltpu.VMEM((1, C), F32),
        pltpu.VMEM((1, C), F32),
        pltpu.VMEM((1, HID), F32),
        pltpu.VMEM((1, C), F32),
        pltpu.VMEM((RH + 6, CW + 16, C), F32),
        pltpu.VMEM((RH + 6, CW + 16, C), F32),
        pltpu.VMEM((RH, CW, C), F32),
        pltpu.VMEM((56, 8, C), F32),
        pltpu.VMEM((C, HID), BF16),
        pltpu.VMEM((HID, C), BF16),
        pltpu.VMEM((RH, CW, C), BF16),
        pltpu.VMEM((8, HID), F32),
        pltpu.VMEM((8, C), F32),
        pltpu.VMEM((448, C), F32),
    ]
    scratch += [
        pltpu.VMEM((2, 3, RH, C), F32),
        pltpu.VMEM((2, 3, RH, C), BF16),
        pltpu.VMEM((2, 3, RH, C), BF16),
    ]
    for _ in range(2):
        scratch += [
            pltpu.VMEM((2, 3, CW, C), BF16),
            pltpu.VMEM((2, 3, RH, C), BF16),
            pltpu.VMEM((4, 3, 16, C), BF16),
        ]
    scratch += [
        pltpu.VMEM((2, C, HID), F32),
        pltpu.VMEM((C, HID), F32),
        pltpu.VMEM((C, HID), F32),
        pltpu.VMEM((XY - 1, 8, HID), F32),
        pltpu.VMEM((NR // 2, 8, HID), F32),
        pltpu.VMEM((2, NC, 8, HID), F32),
        pltpu.VMEM((XY, 4, C), F32),
        pltpu.VMEM((XY - 1, 4, C), F32),
        pltpu.VMEM((NR, 4, C), F32),
        pltpu.VMEM((XY, 4, C), F32),
        sem((10,)), sem((2,)), sem((2,)), sem((8,)), sem((8,)), sem((8,)), sem((8,)), sem((7,)), sem((7,)),
    ]
    shapes = (
        jax.ShapeDtypeStruct((RH, CW, C), BF16),
        jax.ShapeDtypeStruct((RH, CW, C), BF16),
        jax.ShapeDtypeStruct((C // 2, HID), F32),
        jax.ShapeDtypeStruct((HID // 2, C), F32),
        jax.ShapeDtypeStruct((1, HID), F32),
        jax.ShapeDtypeStruct((7, 7, C), F32),
        jax.ShapeDtypeStruct((1, C), F32),
    )
    operands = (
        image[0], dw_kernel, dw_bias.reshape(1, C), layer_norm_gain.reshape(1, C), layer_norm_bias.reshape(1, C),
        w_in, b_in.reshape(1, HID), w_out, b_out.reshape(1, C), cotangent[0],
    )
    outs = pl.pallas_call(
        kernel,
        out_shape=tuple(pltpu.VMEM(x.shape, x.dtype) for x in shapes),
        in_specs=[hbm] * 10,
        out_specs=(pl.BlockSpec(memory_space=pltpu.VMEM),) * 7,
        scratch_shapes=scratch,
        compiler_params=pltpu.CompilerParams(
            collective_id=0, has_side_effects=True, vmem_limit_bytes=48 * 1024 * 1024
        ),
        name="convnext_block",
    )(*[pltpu.with_memory_space_constraint(x, pltpu.HBM) for x in operands])
    outs = pl.pallas_call(
        save,
        out_shape=shapes,
        in_specs=[pl.BlockSpec(memory_space=pl.ANY)] * 7,
        out_specs=(hbm,) * 7,
        scratch_shapes=[sem((7,))],
        name="save_outputs",
    )(*[pltpu.with_memory_space_constraint(x, pltpu.VMEM) for x in outs])
    mixed, d_image, g_in, g_out, g_b, g_k, g_gain = outs
    return (mixed[None], d_image[None], g_in, g_out, g_b.reshape(HID), g_k, g_gain.reshape(C))


def solution(mesh):
    return jax.shard_map(
        on_device,
        mesh=mesh,
        in_specs=(
            P("fsdp", "rows", "cols", None),
            P(),
            P(),
            P(),
            P(),
            P("fsdp", None),
            P(),
            P("fsdp", None),
            P(),
            P("fsdp", "rows", "cols", None),
        ),
        out_specs=(
            P("fsdp", "rows", "cols", None),
            P("fsdp", "rows", "cols", None),
            P("fsdp", None),
            P("fsdp", None),
            P(),
            P(),
            P(),
        ),
        check_vma=False,
    )
```

```python
import functools
import math

import jax
import jax.numpy as jnp
from jax import lax
from jax.experimental import pallas as pl
from jax.experimental.pallas import tpu as pltpu
from jax.sharding import PartitionSpec as P

MESH = pl.DeviceIdType.MESH
F32 = jnp.float32
BF16 = jnp.bfloat16

norm_eps = 1e-06
gelu_coef = math.sqrt(2.0 / math.pi)
cubic_coef = 0.044715

RH = 16
CW = 128
C = 128
HID = 512
XY = 16
NR = 16
NC = 8
PIX = RH * CW

NT = (((1,), (1,)), ((), ()))
TN = (((0,), (0,)), ((), ()))


def tap_sums(source, first, rows, taps, acc, kb, flip):
    for b in range(7):
        weights = [kb[(6 - a) * 8 + (6 - b) if flip else a * 8 + b] for a in range(7)]
        for row in rows:
            value = source[row, pl.ds(first + 5 + b, 8), :]
            for h, a in taps(row):
                acc[h] = acc[h] + value * weights[a]
    return acc


def taps_all(row):
    return [(row - a, a) for a in range(7) if 0 <= row - a < RH]


def kernel(
    image, dw_kernel_in, dw_bias_in, gain_in, bias_in, w_in, b_in_in, w_out, b_out_in, cotangent,
    mixed, dimg, g_in, g_out, g_b, g_k, g_gain,
    img, cot, dw_kernel, dw_bias, gain, bias, b_in, b_out, xp, dp, cv, kb, win, wout, dcb,
    bacc, gacc, kacc,
    wide, hx_side, hd_side, hx_row, hx_col, hx_cor, hd_row, hd_col, hd_cor,
    grads, from_core, pair, r1, r2, a4, small, r1s, r2s, sa,
    local_sem, w_send, w_recv, hx_send, hx_recv, hd_send, hd_recv, x_send, x_recv,
):
    mf = lax.axis_index("fsdp")
    mr = lax.axis_index("rows")
    mc = lax.axis_index("cols")
    me = mf * NC + mc
    core = mr % 2
    other = mr + 1 - 2 * core
    mz = mr // 2

    def xy_id(peer):
        return (peer // NC, mr, peer % NC)

    def row_id(peer):
        return (mf, peer, mc)

    up, down = (mr + NR - 1) % NR, (mr + 1) % NR
    left, right = (mc + NC - 1) % NC, (mc + 1) % NC

    loads = [
        (image, img), (cotangent, cot), (dw_kernel_in, dw_kernel), (dw_bias_in, dw_bias), (gain_in, gain), (bias_in, bias),
        (b_in_in, b_in), (b_out_in, b_out), (w_in, win.at[pl.ds(mf * 64, 64)]), (w_out, wout.at[pl.ds(mf * 256, 256)]),
    ]
    loads = [pltpu.make_async_copy(src, dst, local_sem.at[i]) for i, (src, dst) in enumerate(loads)]
    for i in (2, 3, 0, 1, 4, 5, 6, 7, 8, 9):
        loads[i].start()

    barrier = pltpu.get_barrier_semaphore()

    def greet(device):
        pl.semaphore_signal(barrier, inc=1, device_id=device, device_id_type=MESH)

    def greet_xy(k, _):
        greet(xy_id((me + k) % XY))
        return 0

    def greet_rows(k, _):
        greet(row_id((mr + k) % NR))
        return 0

    def greet_other(k, _):
        greet((mf, other, (mc + k) % NC))
        return 0

    beyond = (mr + NR - 1 + 2 * core) % NR
    greet((mf, beyond, left))
    greet((mf, beyond, right))
    lax.fori_loop(1, NC, greet_other, 0)
    lax.fori_loop(1, XY, greet_xy, 0)
    lax.fori_loop(1, NR, greet_rows, 0)

    loads[2].wait()
    loads[3].wait()
    for a in range(7):
        for b in range(7):
            kb[a * 8 + b] = jnp.broadcast_to(dw_kernel[a, pl.ds(b, 1), :], (8, C))
    conv_bias = jnp.broadcast_to(dw_bias[...], (8, C))

    loads[0].wait()

    def widen(r, _):
        xp[3 + r, pl.ds(8, CW), :] = img[r].astype(F32)
        return 0

    lax.fori_loop(0, RH, widen, 0)

    own_rows = range(3, RH + 3)
    edge_rows = (0, 1, 2, RH + 3, RH + 4, RH + 5)

    def conv_inner(wb, _):
        first = pl.multiple_of(wb * 8, 8)
        acc = tap_sums(xp, first, own_rows, taps_all, [conv_bias] * RH, kb, False)
        for h in range(RH):
            cv[h, pl.ds(first, 8), :] = acc[h]
        return 0

    def pack_sides(padded, wide, packed):
        def row(r, _):
            for j in range(3):
                wide[0, j, pl.ds(r, 1), :] = padded[3 + r, pl.ds(CW + 5 + j, 1), :]
                wide[1, j, pl.ds(r, 1), :] = padded[3 + r, pl.ds(8 + j, 1), :]
            return 0

        lax.fori_loop(0, RH, row, 0)
        packed[...] = wide[...].astype(BF16)

    pack_sides(xp, wide, hx_side)
    lax.fori_loop(1, 4, conv_inner, 0)
    pl.semaphore_wait(barrier, 2 + NC - 1 + XY - 1 + NR - 1)

    def halo(source, sides, rows_buf, col_buf, cor_buf, send, recv):
        plan = [
            (source.at[pl.ds(RH - 3, 3)], rows_buf.at[0], (mf, down, mc)),
            (source.at[pl.ds(0, 3)], rows_buf.at[1], (mf, up, mc)),
            (sides.at[0], col_buf.at[0], (mf, mr, right)),
            (sides.at[1], col_buf.at[1], (mf, mr, left)),
            (source.at[pl.ds(RH - 3, 3), pl.ds(CW - 16, 16)], cor_buf.at[0], (mf, down, right)),
            (source.at[pl.ds(RH - 3, 3), pl.ds(0, 16)], cor_buf.at[1], (mf, down, left)),
            (source.at[pl.ds(0, 3), pl.ds(CW - 16, 16)], cor_buf.at[2], (mf, up, right)),
            (source.at[pl.ds(0, 3), pl.ds(0, 16)], cor_buf.at[3], (mf, up, left)),
        ]
        copies = []
        for i, (src, dst, target) in enumerate(plan):
            copy = pltpu.make_async_remote_copy(
                src_ref=src, dst_ref=dst, send_sem=send.at[i], recv_sem=recv.at[i], device_id=target, device_id_type=MESH
            )
            copy.start()
            copies.append(copy)
        return copies

    has_up = jnp.where(mr > 0, 1.0, 0.0).astype(F32)
    has_down = jnp.where(mr < NR - 1, 1.0, 0.0).astype(F32)
    has_left = jnp.where(mc > 0, 1.0, 0.0).astype(F32)
    has_right = jnp.where(mc < NC - 1, 1.0, 0.0).astype(F32)

    def unpack_halo(padded, wide, rows_buf, col_buf, cor_buf):
        for i in range(3):
            padded[i, pl.ds(8, CW), :] = rows_buf[0, i].astype(F32) * has_up
            padded[RH + 3 + i, pl.ds(8, CW), :] = rows_buf[1, i].astype(F32) * has_down
            padded[i, pl.ds(0, 8), :] = cor_buf[0, i].astype(F32)[8:16] * (has_up * has_left)
            padded[i, pl.ds(CW + 8, 8), :] = cor_buf[1, i].astype(F32)[0:8] * (has_up * has_right)
            padded[RH + 3 + i, pl.ds(0, 8), :] = cor_buf[2, i].astype(F32)[8:16] * (has_down * has_left)
            padded[RH + 3 + i, pl.ds(CW + 8, 8), :] = cor_buf[3, i].astype(F32)[0:8] * (has_down * has_right)

        wide[0] = col_buf[0].astype(F32) * has_left
        wide[1] = col_buf[1].astype(F32) * has_right

        def side(r, _):
            for j in range(3):
                padded[3 + r, pl.ds(5 + j, 1), :] = wide[0, j, pl.ds(r, 1), :]
                padded[3 + r, pl.ds(CW + 8 + j, 1), :] = wide[1, j, pl.ds(r, 1), :]
            return 0

        lax.fori_loop(0, RH, side, 0)

    hx = halo(image, hx_side, hx_row, hx_col, hx_cor, hx_send, hx_recv)
    partner = (1 - mf, mr, mc)
    send_in = pltpu.make_async_remote_copy(
        src_ref=w_in, dst_ref=win.at[pl.ds(mf * 64, 64)], send_sem=w_send.at[0], recv_sem=w_recv.at[0],
        device_id=partner, device_id_type=MESH,
    )
    send_in.start()
    send_out = pltpu.make_async_remote_copy(
        src_ref=w_out, dst_ref=wout.at[pl.ds(mf * 256, 256)], send_sem=w_send.at[1], recv_sem=w_recv.at[1],
        device_id=partner, device_id_type=MESH,
    )
    send_out.start()

    lax.fori_loop(4, CW // 8 - 1, conv_inner, 0)

    for copy in hx:
        copy.wait_recv()
    unpack_halo(xp, wide, hx_row, hx_col, hx_cor)

    def conv_edge(wb, _):
        first = pl.multiple_of(wb * 8, 8)
        acc = [None] * RH
        touched = (0, 1, 2, RH - 3, RH - 2, RH - 1)
        for h in touched:
            acc[h] = cv[h, pl.ds(first, 8), :]
        acc = tap_sums(xp, first, edge_rows, taps_all, acc, kb, False)
        for h in touched:
            cv[h, pl.ds(first, 8), :] = acc[h]
        return 0

    lax.fori_loop(1, CW // 8 - 1, conv_edge, 0)

    def conv_side(i, _):
        first = pl.multiple_of(i * (CW - 8), 8)
        acc = tap_sums(xp, first, range(RH + 6), taps_all, [conv_bias] * RH, kb, False)
        for h in range(RH):
            cv[h, pl.ds(first, 8), :] = acc[h]
        return 0

    lax.fori_loop(0, 2, conv_side, 0)

    for i in (1, 4, 5, 6, 7, 8, 9):
        loads[i].wait()
    send_in.wait_recv()
    send_out.wait_recv()
    def remote(src, dst, sem, device):
        return pltpu.make_async_remote_copy(
            src_ref=src, dst_ref=dst, send_sem=x_send.at[sem], recv_sem=x_recv.at[sem], device_id=device, device_id_type=MESH
        )

    def start(copies):
        for copy in copies:
            copy.start()

    def arrived(ref, sem):
        pltpu.make_async_copy(ref, ref, x_recv.at[sem]).wait()

    def left_here(ref, sem):
        pltpu.make_async_copy(ref, ref, x_send.at[sem]).wait()

    far_xy = (10, 6, 2, 14, 8, 9, 11, 7, 12, 4, 5, 13, 3, 1, 15)
    far_z = (4, 3, 5, 2, 6, 1, 7)
    far_rows = (8, 7, 9, 6, 10, 5, 11, 4, 12, 3, 13, 2, 14, 1, 15)
    far_cols = (6, 2, 4, 5, 7, 3, 1)

    conv = cv[...].reshape(PIX, C)
    center = jnp.mean(conv, axis=-1, keepdims=True)
    spread = conv - center
    rstd = lax.rsqrt(jnp.mean(spread * spread, axis=-1, keepdims=True) + norm_eps)
    xhat = spread * rstd
    normed = (xhat * gain[...] + bias[...]).astype(BF16)
    upstream = cot[...].reshape(PIX, C)
    pre = jnp.dot(normed, win[...], preferred_element_type=F32) + b_in[...]
    square = pre * pre
    tanh_val = jnp.tanh(pre * (gelu_coef + (gelu_coef * cubic_coef) * square))
    half_gate = 0.5 + 0.5 * tanh_val
    hidden = (pre * half_gate).astype(BF16)
    slope = half_gate + (pre * (0.5 - 0.5 * tanh_val * tanh_val)) * (
        gelu_coef + (3.0 * gelu_coef * cubic_coef) * square
    )
    d_wide = lax.dot_general(upstream, wout[...], NT, preferred_element_type=F32) * slope
    d_pre = d_wide.astype(BF16)
    bacc[...] = jnp.sum(d_wide.reshape(PIX // 8, 8, HID), axis=0)

    grads[0] = lax.dot_general(normed, d_pre, TN, preferred_element_type=F32)
    out_turned = lax.dot_general(upstream, hidden, TN, preferred_element_type=F32)
    for q in range(4):
        turned = out_turned[:, q * 128 : (q + 1) * 128].T
        for u in range(16):
            p, at = q * 4 + u // 4, u % 4
            grads[1, p * 8 : (p + 1) * 8, at * 128 : (at + 1) * 128] = turned[u * 8 : (u + 1) * 8]

    dn = lax.dot_general(d_pre, win[...], NT, preferred_element_type=F32)
    gacc[...] = jnp.sum((dn * xhat).reshape(PIX // 8, 8, C), axis=0)
    q = dn * gain[...]
    d_conv = (
        rstd * (q - jnp.mean(q, axis=-1, keepdims=True) - xhat * jnp.mean(q * xhat, axis=-1, keepdims=True))
    ).astype(BF16)
    d_rows = d_conv.reshape(RH, CW, C)
    dcb[...] = d_rows
    dp[pl.ds(3, RH), pl.ds(8, CW), :] = d_rows.astype(F32)

    start([remote(grads.at[1 - core], from_core, 0, (mf, other, mc))])
    pack_sides(dp, wide, hd_side)
    hd = halo(dcb, hd_side, hd_row, hd_col, hd_cor, hd_send, hd_recv)

    def send_pair():
        arrived(from_core, 0)

        def add(p, _):
            rows = pl.ds(pl.multiple_of(p * 8, 8), 8)
            pair[rows, :] = grads[core, rows, :] + from_core[rows, :]
            return 0

        lax.fori_loop(0, XY, add, 0)
        copies = []
        for k in far_xy:
            peer = (me + k) % XY
            rows = pl.ds(pl.multiple_of(peer * 8, 8), 8)
            copies.append(remote(pair.at[rows], r1.at[k - 1], 1, xy_id(peer)))
        start(copies)

    def send_sums():
        arrived(r1, 1)
        total = pair[pl.ds(pl.multiple_of(me * 8, 8), 8), :]
        for k in range(XY - 1):
            total = total + r1[k]
        r2[mz] = total
        start([remote(r2.at[mz], r2.at[mz], 2, row_id((mr + 2 * k) % NR)) for k in far_z])

    def send_result():
        arrived(r2.at[pl.ds(0, NR // 2 - 1)], 2)
        total = r2[0]
        for z in range(1, NR // 2):
            total = total + r2[z]
        a4[core, mc] = total
        copies = []
        for k in far_cols:
            for row in (other, mr):
                copies.append(remote(a4.at[core, mc], a4.at[core, mc], 3, (mf, row, (mc + k) % NC)))
        copies.append(remote(a4.at[core, mc], a4.at[core, mc], 3, (mf, other, mc)))
        start(copies)

    def send_small():
        start([remote(small.at[(me + k) % XY], r1s.at[k - 1], 4, xy_id((me + k) % XY)) for k in far_xy])

    def send_small_sums():
        arrived(r1s, 4)
        total = small[me]
        for k in range(XY - 1):
            total = total + r1s[k]
        r2s[mr] = total
        start([remote(r2s.at[mr], r2s.at[mr], 5, row_id((mr + k) % NR)) for k in far_rows])

    def send_small_result():
        arrived(r2s.at[pl.ds(0, NR - 1)], 5)
        total = r2s[0]
        for r in range(1, NR):
            total = total + r2s[r]
        sa[me] = total
        start([remote(sa.at[me], sa.at[me], 6, xy_id((me + k) % XY)) for k in far_xy])

    def tap_gradient(taps, unroll):
        def step(wb, acc):
            first = pl.multiple_of(wb * 8, 8)
            acc = list(acc)
            grad = [dp[3 + h, pl.ds(first + 8, 8), :] for h in range(RH)]
            for i, b in enumerate(taps):
                for row in range(RH + 6):
                    value = xp[row, pl.ds(first + 5 + b, 8), :]
                    for h, a in taps_all(row):
                        acc[i * 7 + a] = acc[i * 7 + a] + value * grad[h]
            return tuple(acc)

        zero = jnp.zeros((8, C), F32)
        acc = lax.fori_loop(0, CW // 8, step, (zero,) * (7 * len(taps)), unroll=unroll)
        for i, b in enumerate(taps):
            for a in range(7):
                kacc[pl.ds((a * 8 + b) * 8, 8), :] = acc[i * 7 + a]

    tap_gradient((0, 1), 2)
    send_pair()
    tap_gradient((2, 3), 2)
    tap_gradient((4, 5), 2)
    tap_gradient((6,), 4)
    for a in range(7):
        kacc[pl.ds((a * 8 + 7) * 8, 8), :] = jnp.zeros((8, C), F32)
    for a in range(7):
        total = kacc[pl.ds(a * 64, 8, stride=8), :]
        for s in range(1, 8):
            total = total + kacc[pl.ds(a * 64 + s, 8, stride=8), :]
        small[2 * a] = total[0:4]
        small[2 * a + 1] = total[4:8]
    for q in range(4):
        small[14, pl.ds(q, 1), :] = jnp.sum(bacc[:, q * 128 : (q + 1) * 128], axis=0, keepdims=True)
    small[15] = jnp.broadcast_to(jnp.sum(gacc[...], axis=0, keepdims=True), (4, C))
    send_small()


    for copy in hd:
        copy.wait_recv()
    unpack_halo(dp, wide, hd_row, hd_col, hd_cor)

    def image_gradient(wb, _):
        first = pl.multiple_of(wb * 8, 8)
        acc = tap_sums(dp, first, range(RH + 6), taps_all, [jnp.zeros((8, C), F32)] * RH, kb, True)
        for h in range(RH):
            cv[h, pl.ds(first, 8), :] = acc[h]
        return 0

    def finish(wb, _):
        first = pl.multiple_of(wb * 16, 16)
        columns = pl.ds(first, 16)
        for h in range(RH):
            dimg[h, columns, :] = (cot[h, columns, :].astype(F32) + cv[h, columns, :]).astype(BF16)
        return 0

    lax.fori_loop(0, 4, image_gradient, 0)
    send_sums()
    lax.fori_loop(4, 8, image_gradient, 0)
    send_small_sums()
    lax.fori_loop(8, 16, image_gradient, 0)
    send_result()
    send_small_result()
    out_sum = jnp.dot(hidden, wout[...], preferred_element_type=F32)
    field = img[...].reshape(PIX, C).astype(F32)
    mixed[...] = (field + out_sum + b_out[...]).astype(BF16).reshape(RH, CW, C)
    lax.fori_loop(0, 8, finish, 0)

    arrived(r1, 3)
    def place(j, _):
        for q in range(4):
            at = pl.multiple_of(j * 32 + q * 8, 8)
            g_out[pl.ds(at, 8), :] = a4[1, j, :, q * 128 : (q + 1) * 128]
        g_in[pl.ds(pl.multiple_of(j * 8, 8), 8), :] = a4[0, j]
        return 0

    lax.fori_loop(0, NC, place, 0)
    arrived(sa.at[pl.ds(0, XY - 1)], 6)
    for a in range(7):
        g_k[a, pl.ds(0, 4), :] = sa[2 * a]
        g_k[a, pl.ds(4, 3), :] = sa[2 * a + 1][0:3]
    for q in range(4):
        g_b[:, q * 128 : (q + 1) * 128] = sa[14, pl.ds(q, 1), :]
    g_gain[...] = sa[15, pl.ds(0, 1), :]

    for copy in hx:
        copy.wait_send()
    for copy in hd:
        copy.wait_send()
    send_in.wait_send()
    send_out.wait_send()
    left_here(from_core, 0)
    left_here(r1, 1)
    left_here(r2.at[pl.ds(0, NR // 2 - 1)], 2)
    left_here(r1, 3)
    left_here(r1s, 4)
    left_here(r2s.at[pl.ds(0, NR - 1)], 5)
    left_here(sa.at[pl.ds(0, XY - 1)], 6)


def save(*refs):
    sources, targets, sem = refs[:7], refs[7:14], refs[14]
    copies = [pltpu.make_async_copy(src, dst, sem.at[i]) for i, (src, dst) in enumerate(zip(sources, targets))]
    for copy in copies:
        copy.start()
    for copy in copies:
        copy.wait()


def on_device(
    image, dw_kernel, dw_bias, layer_norm_gain, layer_norm_bias, w_in, b_in, w_out, b_out, cotangent
):
    hbm = pl.BlockSpec(memory_space=pltpu.HBM)
    sem = pltpu.SemaphoreType.DMA
    scratch = [
        pltpu.VMEM((RH, CW, C), BF16),
        pltpu.VMEM((RH, CW, C), BF16),
        pltpu.VMEM((7, 7, C), F32),
        pltpu.VMEM((1, C), F32),
        pltpu.VMEM((1, C), F32),
        pltpu.VMEM((1, C), F32),
        pltpu.VMEM((1, HID), F32),
        pltpu.VMEM((1, C), F32),
        pltpu.VMEM((RH + 6, CW + 16, C), F32),
        pltpu.VMEM((RH + 6, CW + 16, C), F32),
        pltpu.VMEM((RH, CW, C), F32),
        pltpu.VMEM((56, 8, C), F32),
        pltpu.VMEM((C, HID), BF16),
        pltpu.VMEM((HID, C), BF16),
        pltpu.VMEM((RH, CW, C), BF16),
        pltpu.VMEM((8, HID), F32),
        pltpu.VMEM((8, C), F32),
        pltpu.VMEM((448, C), F32),
    ]
    scratch += [
        pltpu.VMEM((2, 3, RH, C), F32),
        pltpu.VMEM((2, 3, RH, C), BF16),
        pltpu.VMEM((2, 3, RH, C), BF16),
    ]
    for _ in range(2):
        scratch += [
            pltpu.VMEM((2, 3, CW, C), BF16),
            pltpu.VMEM((2, 3, RH, C), BF16),
            pltpu.VMEM((4, 3, 16, C), BF16),
        ]
    scratch += [
        pltpu.VMEM((2, C, HID), F32),
        pltpu.VMEM((C, HID), F32),
        pltpu.VMEM((C, HID), F32),
        pltpu.VMEM((XY - 1, 8, HID), F32),
        pltpu.VMEM((NR // 2, 8, HID), F32),
        pltpu.VMEM((2, NC, 8, HID), F32),
        pltpu.VMEM((XY, 4, C), F32),
        pltpu.VMEM((XY - 1, 4, C), F32),
        pltpu.VMEM((NR, 4, C), F32),
        pltpu.VMEM((XY, 4, C), F32),
        sem((10,)), sem((2,)), sem((2,)), sem((8,)), sem((8,)), sem((8,)), sem((8,)), sem((7,)), sem((7,)),
    ]
    shapes = (
        jax.ShapeDtypeStruct((RH, CW, C), BF16),
        jax.ShapeDtypeStruct((RH, CW, C), BF16),
        jax.ShapeDtypeStruct((C // 2, HID), F32),
        jax.ShapeDtypeStruct((HID // 2, C), F32),
        jax.ShapeDtypeStruct((1, HID), F32),
        jax.ShapeDtypeStruct((7, 7, C), F32),
        jax.ShapeDtypeStruct((1, C), F32),
    )
    operands = (
        image[0], dw_kernel, dw_bias.reshape(1, C), layer_norm_gain.reshape(1, C), layer_norm_bias.reshape(1, C),
        w_in, b_in.reshape(1, HID), w_out, b_out.reshape(1, C), cotangent[0],
    )
    outs = pl.pallas_call(
        kernel,
        out_shape=tuple(pltpu.VMEM(x.shape, x.dtype) for x in shapes),
        in_specs=[hbm] * 10,
        out_specs=(pl.BlockSpec(memory_space=pltpu.VMEM),) * 7,
        scratch_shapes=scratch,
        compiler_params=pltpu.CompilerParams(
            collective_id=0, has_side_effects=True, vmem_limit_bytes=48 * 1024 * 1024
        ),
        name="convnext_block",
    )(*[pltpu.with_memory_space_constraint(x, pltpu.HBM) for x in operands])
    outs = pl.pallas_call(
        save,
        out_shape=shapes,
        in_specs=[pl.BlockSpec(memory_space=pl.ANY)] * 7,
        out_specs=(hbm,) * 7,
        scratch_shapes=[sem((7,))],
        name="save_outputs",
    )(*[pltpu.with_memory_space_constraint(x, pltpu.VMEM) for x in outs])
    mixed, d_image, g_in, g_out, g_b, g_k, g_gain = outs
    return (mixed[None], d_image[None], g_in, g_out, g_b.reshape(HID), g_k, g_gain.reshape(C))


def solution(mesh):
    return jax.shard_map(
        on_device,
        mesh=mesh,
        in_specs=(
            P("fsdp", "rows", "cols", None),
            P(),
            P(),
            P(),
            P(),
            P("fsdp", None),
            P(),
            P("fsdp", None),
            P(),
            P("fsdp", "rows", "cols", None),
        ),
        out_specs=(
            P("fsdp", "rows", "cols", None),
            P("fsdp", "rows", "cols", None),
            P("fsdp", None),
            P("fsdp", None),
            P(),
            P(),
            P(),
        ),
        check_vma=False,
    )
```
